128 devices in a mesh: tile: 8 (over z, y_lo), pos: 16 (over y_hi, x, core).
Axes of the slice: x: 4, y: 4 (y_hi: 2, y_lo: 2; y = y_hi * 2 + y_lo), z: 4, core: 2. Of those that a mesh axis runs over, the one named last changes fastest.
Arguments:
- object_field: float32 [2, 4096, 8192], P(None, 'tile', 'pos'), may hold values from -5 to 5
- probe_field: float32 [2, 512, 512], replicated, may hold values from -5 to 5
- offsets: int32 [8, 16, 3, 2], P('tile', 'pos'), may hold values from 0 to 511, as said below
- counts: int32 [8, 16], P('tile'), may hold values from 1 to 3, as said below
- intensity: float32 [8, 16, 3, 512, 512], P('tile', 'pos'), may hold values from 0 to 2
Outputs:
- object_grad: float32 [2, 4096, 8192], P(None, 'tile', 'pos')
- probe_grad: float32 [2, 512, 512], replicated
The draws below stay inside these ranges and needn't reach their ends.
Inputs may be any that keep to these rules, and one draw needn't show every extreme that they name: `offsets`: offsets are local to the device's block. On the last index of tile the row offset is at most 0, on the last index of pos the column offset likewise, so every window lies inside the object. Offsets of unused slots are drawn too and mean nothing. `counts`: some device uses all 3 slots and some uses one; the used slots of a device are its first ones.
All inputs are finite; a program needn't handle non-finite values.
Results may differ from the reference program's by a relative error of at most 0.0003.
Values sent between devices are 32-bit elements; how exact they have to be, the bound alone decides.
A program may use at most 128 MiB of HBM per device.

```python
import jax
import jax.numpy as jnp
from jax import lax

WIN = 512
BLOCK = 512
SLOTS = 3
NROWS = 4096
NCOLS = 8192
N_TILE = 8
N_POS = 16


def draw_offsets(key, part):
    key = jax.random.fold_in(key, 11)
    key_rows, key_cols = jax.random.split(key)
    tile_ids = jnp.arange(N_TILE, dtype=jnp.int32)[:, None, None]
    column_ids = jnp.arange(N_POS, dtype=jnp.int32)[None, :, None]
    filler = jnp.zeros((N_TILE, N_POS, SLOTS), jnp.int32)
    row_limit = jnp.where(tile_ids == N_TILE - 1, BLOCK - WIN + 1, BLOCK) + filler
    col_limit = jnp.where(column_ids == N_POS - 1, BLOCK - WIN + 1, BLOCK) + filler
    row_offset = jax.random.randint(key_rows, (N_TILE, N_POS, SLOTS), 0, row_limit)
    col_offset = jax.random.randint(key_cols, (N_TILE, N_POS, SLOTS), 0, col_limit)
    row_offset = row_offset.at[0, 0, 0].set(BLOCK - 1).at[N_TILE - 1, N_POS - 1, 0].set(0)
    col_offset = col_offset.at[0, 0, 0].set(BLOCK - 1).at[N_TILE - 1, N_POS - 1, 0].set(0)
    return jnp.stack([row_offset, col_offset], axis=-1).astype(jnp.int32)


def draw_counts(key, part):
    key = jax.random.fold_in(key, 23)
    drawn = jax.random.randint(key, (N_TILE, N_POS), 1, SLOTS + 1)
    drawn = drawn.at[0, 1].set(SLOTS).at[1, 0].set(1)
    return drawn.astype(jnp.int32)


def block_levels(own_key, extent, cuts, smallest, high):
    gain = 1.0
    for position, blocks in cuts:
        heights = jax.random.uniform(jax.random.fold_in(jax.random.fold_in(own_key, 6), position), (blocks,), jnp.float32, smallest / len(cuts), high / len(cuts))
        gain = gain * jnp.repeat(jnp.exp(heights), extent[position] // blocks).reshape((-1,) + (1,) * (len(extent) - 1 - position))
    return gain


def normal_values(own_key, dims, width, bound, cuts=(), kind=jnp.bfloat16):
    result = width * jax.random.normal(own_key, dims, jnp.float32)
    if cuts:
        result = result * block_levels(own_key, dims, cuts, -0.22, 0.18)
    return jnp.clip(result, -bound, bound).astype(kind)


def setup_inputs(seed: int = 0) -> dict:
    arg_keys = jax.random.split(jax.random.key(seed), 6)
    object_field = normal_values(arg_keys[0], (2, NROWS, NCOLS), 0.7, 5.0, ((1, 8), (2, 16)), jnp.float32)
    probe_field = normal_values(arg_keys[1], (2, WIN, WIN), 0.7, 5.0, (), jnp.float32)
    offsets = draw_offsets(jax.random.fold_in(arg_keys[5], 71), 0)
    counts = draw_counts(jax.random.fold_in(arg_keys[5], 71), 0)
    intensity = jnp.clip(2.0 * jax.random.uniform(arg_keys[4], (N_TILE, N_POS, SLOTS, WIN, WIN), jnp.float32) ** block_levels(arg_keys[4], (N_TILE, N_POS, SLOTS, WIN, WIN), ((0, 8), (1, 16)), -0.2, 0.2), 0.0, 2.0)
    return {"object_field": object_field, "probe_field": probe_field, "offsets": offsets, "counts": counts, "intensity": intensity}


def slot_terms(patch_real, patch_imag, probe_field, measured):
    probe_wave = probe_field[0] + 1j * probe_field[1]
    object_wave = patch_real + 1j * patch_imag
    spectrum = jnp.fft.fft2(probe_wave * object_wave, norm="ortho")
    mismatch = spectrum.real * spectrum.real + spectrum.imag * spectrum.imag - measured
    back_wave = jnp.fft.ifft2(mismatch * spectrum, norm="ortho")
    object_term = jnp.conj(probe_wave) * back_wave
    probe_term = jnp.conj(object_wave) * back_wave
    return (jnp.stack([object_term.real, object_term.imag]),
            jnp.stack([probe_term.real, probe_term.imag]))


def reference(object_field, probe_field, offsets, counts, intensity):
    zero_int = jnp.zeros((), jnp.int32)

    def visit_slot(state, flat_index):
        tile_index = flat_index // (N_POS * SLOTS)
        column_index = (flat_index // SLOTS) % N_POS
        slot_index = flat_index % SLOTS
        row_start = (tile_index * BLOCK + offsets[tile_index, column_index, slot_index, 0]).astype(jnp.int32)
        col_start = (column_index * BLOCK + offsets[tile_index, column_index, slot_index, 1]).astype(jnp.int32)

        def accumulate(inner):
            grad_now, probe_now = inner
            corner = (zero_int, row_start, col_start)
            patch_now = lax.dynamic_slice(object_field, corner, (2, WIN, WIN))
            object_term, probe_term = slot_terms(patch_now[0], patch_now[1], probe_field,
                                                 intensity[tile_index, column_index, slot_index])
            window_now = lax.dynamic_slice(grad_now, corner, (2, WIN, WIN))
            grad_now = lax.dynamic_update_slice(grad_now, window_now + object_term, corner)
            return (grad_now, probe_now + probe_term)

        def untouched(inner):
            return inner

        slot_used = slot_index < counts[tile_index, column_index]
        return lax.cond(slot_used, accumulate, untouched, state), None

    start_state = (jnp.zeros(object_field.shape, jnp.float32), jnp.zeros(probe_field.shape, jnp.float32))
    final_state, ignored = lax.scan(visit_slot, start_state, jnp.arange(N_TILE * N_POS * SLOTS, dtype=jnp.int32))
    object_grad, probe_sum = final_state
    return object_grad, probe_sum * (1.0 / (N_TILE * N_POS * SLOTS))
```

```python
import functools
import math

import jax
import jax.numpy as jnp
import numpy as np
from jax import lax
from jax.experimental import pallas as pl
from jax.experimental.pallas import tpu as pltpu
from jax.sharding import PartitionSpec as P

MESH = pl.DeviceIdType.MESH
WIN = 512
SLOTS = 3
ROWS = 64
CHUNKS = WIN // ROWS
LAG = 2
TILES = 8
COLS = 16
SEAM = 8
QUARTER = WIN // 4
SLAB = 256
RIGHT, LOWER, CORNER = 0, 1, 2
F32 = jnp.float32
BF16 = jnp.bfloat16


def split_table(table):
    high = table.astype(BF16)
    low = (table - high.astype(np.float64)).astype(BF16)
    return high, low


def row_tables():
    points = np.arange(WIN)
    angles = (points[:, None] * points[None, :] % WIN) * (2.0 * math.pi / WIN)
    stacked = np.concatenate([np.cos(angles), np.sin(angles)], axis=0) / math.sqrt(WIN)
    return split_table(stacked)


def column_tables():
    blocks = []
    for residue in range(4):
        freqs = 4 * np.arange(QUARTER) + residue
        angles = (freqs[:, None] * np.arange(QUARTER)[None, :] % WIN) * (2.0 * math.pi / WIN)
        cosine = np.cos(angles) / math.sqrt(WIN)
        sine = np.sin(angles) / math.sqrt(WIN)
        blocks.append(np.block([[cosine, sine], [-sine, cosine]]))
    forward = np.stack(blocks)
    backward = np.swapaxes(forward, 1, 2)
    return split_table(np.stack([forward, backward]))


def split_value(value):
    high = value.astype(BF16)
    low = (value - high.astype(F32)).astype(BF16)
    return high, low


def dot(left, right):
    return jnp.dot(left, right, preferred_element_type=F32)


def one_hot(shape, axis, base, amount):
    along = lax.broadcasted_iota(jnp.int32, shape, axis)
    other = lax.broadcasted_iota(jnp.int32, shape, 1 - axis)
    return jnp.where(along == ((other + (base + amount)) & (WIN - 1)), 1.0, 0.0).astype(BF16)


def chunk_rows(k):
    return pl.ds(pl.multiple_of(k * ROWS, ROWS), ROWS)


def device_at(z, y, x, core):
    return (z * 2 + y % 2, ((y // 2) * 4 + x) * 2 + core)


def kernel(
    place, counts, obj, probe, inten, row_hi, row_lo, col_hi, col_lo,
    out_obj, out_probe,
    own, halo, grad, back, spec, turned, term_hi, term_lo, roll_cols, unroll_cols, measured,
    wh, wl, ch, cl, left_hi, left_lo,
    probe_sum, pair_in, z_in, plane_in, gathered,
    load_sem, out_sem,
    up_s, up_r, side_s, side_r, cor_s, cor_r,
    gb_s, gb_r, gc_s, gc_r, gd_s, gd_r,
    pair_s, pair_r, z_s, z_r, plane_s, plane_r, ag_s, ag_r, zg_s, zg_r, pg_s, pg_r,
):
    t = lax.axis_index("tile")
    p = lax.axis_index("pos")
    z = t // 2
    core = p % 2
    x = (p // 2) % 4
    y = (p // 8) * 2 + t % 2
    plane_me = y * 4 + x
    own_count = counts[p]
    partner = (t, p + 1 - 2 * core)

    loads = [
        pltpu.make_async_copy(obj, own, load_sem.at[0]),
        pltpu.make_async_copy(probe, probe_sum, load_sem.at[1]),
        pltpu.make_async_copy(row_hi, wh, load_sem.at[2]),
        pltpu.make_async_copy(row_lo, wl, load_sem.at[3]),
        pltpu.make_async_copy(col_hi, ch, load_sem.at[4]),
        pltpu.make_async_copy(col_lo, cl, load_sem.at[5]),
    ]
    for lanes in range(4):
        loads.append(
            pltpu.make_async_copy(
                inten.at[:, :, pl.ds(lanes * QUARTER, QUARTER)], measured.at[lanes],
                load_sem.at[6 + lanes],
            )
        )
    for load in loads:
        load.start()

    barrier = pltpu.get_barrier_semaphore()

    def greet(device):
        pl.semaphore_signal(barrier, inc=1, device_id=device, device_id_type=MESH)

    t_up = (t + TILES - 1) % TILES
    t_down = (t + 1) % TILES
    p_left = (p + COLS - 1) % COLS
    p_right = (p + 1) % COLS
    for device in (
        (t_up, p), (t_down, p), (t, p_left), (t, p_right), (t_up, p_left), (t_down, p_right),
    ):
        greet(device)
    for step in range(1, 4):
        greet(device_at((z + step) % 4, y, x, core))

    def greet_plane(step, carry):
        peer = (plane_me + step) % 16
        greet(device_at(z, peer // 4, peer % 4, core))
        return carry

    lax.fori_loop(1, 16, greet_plane, 0)
    pl.semaphore_wait(barrier, 6 + 3 + 15)

    def remote(source, target, send, recv, device):
        return pltpu.make_async_remote_copy(
            src_ref=source, dst_ref=target, send_sem=send, recv_sem=recv,
            device_id=device, device_id_type=MESH,
        )

    def up_copy(k):
        rows = chunk_rows(k)
        return remote(
            obj.at[:, rows, :], halo.at[LOWER, :, rows, :], up_s.at[k], up_r.at[k], (t_up, p)
        )

    def side_copy(k):
        rows = chunk_rows(k)
        return remote(
            obj.at[:, rows, :], halo.at[RIGHT, :, rows, :], side_s.at[k], side_r.at[k], (t, p_left)
        )

    def corner_copy(k):
        rows = chunk_rows(k)
        return remote(
            halo.at[LOWER, :, rows, :], halo.at[CORNER, :, rows, :], cor_s.at[k], cor_r.at[k],
            (t, p_left),
        )

    def corner_direct(k):
        rows = chunk_rows(k)
        return remote(
            obj.at[:, rows, :], halo.at[CORNER, :, rows, :], cor_s.at[k], cor_r.at[k],
            (t_up, p_left),
        )

    def grad_side(k):
        rows = chunk_rows(k)
        return remote(
            grad.at[1, :, rows, :], back.at[RIGHT, :, rows, :], gb_s.at[k], gb_r.at[k],
            (t, p_right),
        )

    def grad_down(k):
        rows = chunk_rows(k)
        return remote(
            grad.at[2, :, rows, :], back.at[LOWER, :, rows, :], gc_s.at[k], gc_r.at[k],
            (t_down, p),
        )

    def grad_corner(k):
        rows = chunk_rows(k)
        return remote(
            grad.at[3, :, rows, :], back.at[CORNER, :, rows, :], gd_s.at[k], gd_r.at[k],
            (t, p_right),
        )

    def grad_corner_direct(k):
        rows = chunk_rows(k)
        return remote(
            grad.at[3, :, rows, :], back.at[CORNER, :, rows, :], gd_s.at[k], gd_r.at[k],
            (t_down, p_right),
        )

    has_up = t > 0
    has_down = t < TILES - 1
    has_left = p > 0
    has_right = p < COLS - 1
    after_seam = p == SEAM
    before_seam = p == SEAM - 1
    passes_on = has_left & has_down & jnp.logical_not(after_seam)

    def first_sends(k, carry):
        @pl.when(has_up)
        def _():
            up_copy(k).start()

        @pl.when(has_left)
        def _():
            side_copy(k).start()

        @pl.when(has_up & after_seam)
        def _():
            corner_direct(k).start()

        return carry

    lax.fori_loop(0, CHUNKS, first_sends, 0)

    for load in loads[:4]:
        load.wait()

    for part in range(2):
        high, low = split_value(probe_sum[part])
        term_hi[pl.ds(0, WIN), pl.ds(part * WIN, WIN)] = high
        term_lo[pl.ds(0, WIN), pl.ds(part * WIN, WIN)] = low

    def build_rolls(s, carry):
        amount = place[2 * s + 1]
        roll_cols[s] = one_hot((WIN, WIN), 1, 0, amount)
        unroll_cols[s] = one_hot((WIN, WIN), 0, 0, amount)
        return carry

    lax.fori_loop(0, SLOTS, build_rolls, 0)

    def roll_probe(step, carry):
        s = step // 4
        base = (step % 4) * QUARTER
        rows = pl.ds(pl.multiple_of(base, QUARTER), QUARTER)
        pick = one_hot((QUARTER, WIN), 1, base, WIN - place[2 * s])
        for part in range(2):
            columns = pl.ds(part * WIN, WIN)
            moved = dot(pick, term_hi[pl.ds(0, WIN), columns])
            moved += dot(pick, term_lo[pl.ds(0, WIN), columns])
            high, low = split_value(moved)
            turned[s, part, rows, :] = dot(high, roll_cols[s]) + dot(low, roll_cols[s])
        return carry

    lax.fori_loop(0, SLOTS * 4, roll_probe, 0)

    row_iota = lax.broadcasted_iota(jnp.int32, (ROWS, WIN), 0)
    col_iota = lax.broadcasted_iota(jnp.int32, (ROWS, WIN), 1)

    def slot_masks(s, k):
        above = (row_iota + k * ROWS) < place[2 * s]
        before = col_iota < place[2 * s + 1]
        return above, before

    def patch_part(part, rows, above, before):
        upper = jnp.where(before, halo[RIGHT, part, rows, :], own[part, rows, :])
        lower = jnp.where(before, halo[CORNER, part, rows, :], halo[LOWER, part, rows, :])
        return jnp.where(above, lower, upper)

    def put_left(s, real, imag, sign):
        top = pl.ds(s * ROWS, ROWS)
        low_rows = pl.ds((SLOTS + s) * ROWS, ROWS)
        first = pl.ds(0, WIN)
        second = pl.ds(WIN, WIN)
        for ref, re, im in zip((left_hi, left_lo), split_value(real), split_value(imag)):
            ref[top, first] = re
            ref[low_rows, first] = im
            if sign > 0:
                ref[top, second] = im
                ref[low_rows, second] = -re
            else:
                ref[top, second] = -im
                ref[low_rows, second] = re

    def row_transform(cols):
        columns = pl.ds(cols * SLAB, SLAB)
        high = left_hi[...]
        table = wh[:, columns]
        total = dot(high, table)
        total = total + dot(left_lo[...], table)
        return total + dot(high, wl[:, columns])

    def forward_chunk(k):
        rows = chunk_rows(k)
        for s in range(SLOTS):
            above, before = slot_masks(s, k)
            re = patch_part(0, rows, above, before)
            im = patch_part(1, rows, above, before)
            pr = turned[s, 0, rows, :]
            pi = turned[s, 1, rows, :]
            put_left(s, pr * re - pi * im, pr * im + pi * re, 1)
        for cols in range(WIN // SLAB):
            total = row_transform(cols)
            for s in range(SLOTS):
                for part in range(2):
                    base = (part * SLOTS + s) * ROWS
                    spec[s, part, rows, pl.ds(cols * SLAB, SLAB)] = total[base:base + ROWS]

    def forward_step(j, carry):
        @pl.when(j < CHUNKS)
        def _():
            @pl.when(has_down)
            def _():
                up_copy(j).wait_recv()

            @pl.when(passes_on)
            def _():
                corner_copy(j).start()

        @pl.when(j >= LAG)
        def _():
            k = j - LAG

            @pl.when(has_right)
            def _():
                side_copy(k).wait_recv()

            @pl.when(has_right & has_down)
            def _():
                corner_copy(k).wait_recv()

            forward_chunk(k)

        return carry

    lax.fori_loop(0, CHUNKS + LAG, forward_step, 0)

    for load in loads[4:]:
        load.wait()

    def middle(step, carry):
        s = step // (WIN // SLAB)
        slab = step % (WIN // SLAB)
        columns = pl.ds(pl.multiple_of(slab * SLAB, SLAB), SLAB)

        def quarter(part, j):
            return spec[s, part, pl.ds(j * QUARTER, QUARTER), columns]

        re = [quarter(0, j) for j in range(4)]
        im = [quarter(1, j) for j in range(4)]
        er, ei = re[0] + re[2], im[0] + im[2]
        fr, fi = re[0] - re[2], im[0] - im[2]
        gr, gi = re[1] + re[3], im[1] + im[3]
        hr, hi = re[1] - re[3], im[1] - im[3]
        mixed = [
            (er + gr, ei + gi), (fr + hi, fi - hr), (er - gr, ei - gi), (fr - hi, fi + hr),
        ]
        outs = []
        for q in range(4):
            high, low = split_value(jnp.concatenate(mixed[q], axis=0))
            total = dot(ch[0, q], high) + dot(cl[0, q], high) + dot(ch[0, q], low)
            sr, si = total[:QUARTER], total[QUARTER:]
            levels = [measured[2 * slab + n, s, pl.ds(q, QUARTER, stride=4), :] for n in range(2)]
            miss = sr * sr + si * si - jnp.concatenate(levels, axis=1)
            high, low = split_value(jnp.concatenate([miss * sr, miss * si], axis=0))
            total = dot(ch[1, q], high) + dot(cl[1, q], high) + dot(ch[1, q], low)
            outs.append((total[:QUARTER], total[QUARTER:]))
        (ar, ai), (br, bi), (cr, ci), (dr, di) = outs
        er, ei = ar + cr, ai + ci
        fr, fi = ar - cr, ai - ci
        gr, gi = br + dr, bi + di
        hr, hi = br - dr, bi - di
        results = [
            (er + gr, ei + gi), (fr - hi, fi + hr), (er - gr, ei - gi), (fr + hi, fi - hr),
        ]
        for j in range(4):
            for part in range(2):
                spec[s, part, pl.ds(j * QUARTER, QUARTER), columns] = results[j][part]
        return carry

    lax.fori_loop(0, SLOTS * (WIN // SLAB), middle, 0)

    def backward_chunk(k):
        rows = chunk_rows(k)
        for s in range(SLOTS):
            put_left(s, spec[s, 0, rows, :], spec[s, 1, rows, :], -1)
        for cols in range(WIN // SLAB):
            total = row_transform(cols)
            for s in range(SLOTS):
                for part in range(2):
                    base = (part * SLOTS + s) * ROWS
                    spec[s, part, rows, pl.ds(cols * SLAB, SLAB)] = total[base:base + ROWS]
        zero = jnp.zeros((ROWS, WIN), F32)
        sums = [[zero, zero] for _ in range(4)]
        for s in range(SLOTS):
            used = own_count > s
            above, before = slot_masks(s, k)
            br = spec[s, 0, rows, :]
            bi = spec[s, 1, rows, :]
            pr = turned[s, 0, rows, :]
            pi = turned[s, 1, rows, :]
            terms = (pr * br + pi * bi, pr * bi - pi * br)
            for part in range(2):
                term = jnp.where(used, terms[part], zero)
                lower = jnp.where(above, term, zero)
                upper = term - lower
                upper_right = jnp.where(before, upper, zero)
                lower_right = jnp.where(before, lower, zero)
                sums[0][part] += upper - upper_right
                sums[1][part] += upper_right
                sums[2][part] += lower - lower_right
                sums[3][part] += lower_right
            re = patch_part(0, rows, above, before)
            im = patch_part(1, rows, above, before)
            terms = (re * br + im * bi, re * bi - im * br)
            high, low = split_value(jnp.where(used, jnp.concatenate(terms, axis=0), 0.0))
            moved = dot(high, unroll_cols[s]) + dot(low, unroll_cols[s])
            high, low = split_value(moved)
            term_rows = pl.ds(pl.multiple_of(s * WIN + k * ROWS, ROWS), ROWS)
            for part in range(2):
                columns = pl.ds(part * WIN, WIN)
                term_hi[term_rows, columns] = high[part * ROWS:(part + 1) * ROWS]
                term_lo[term_rows, columns] = low[part * ROWS:(part + 1) * ROWS]
        for block in range(4):
            for part in range(2):
                grad[block, part, rows, :] = sums[block][part]

    receives_corner = has_left & jnp.logical_not(after_seam) & has_down

    def add_down(k):
        rows = chunk_rows(k)

        @pl.when(receives_corner)
        def _():
            grad_corner(k).wait_recv()
            for part in range(2):
                grad[2, part, rows, :] += back[CORNER, part, rows, :]

        @pl.when(has_down)
        def _():
            grad_down(k).start()

    def backward_step(j, carry):
        @pl.when(j < CHUNKS)
        def _():
            backward_chunk(j)

            @pl.when(has_right & has_down & jnp.logical_not(before_seam))
            def _():
                grad_corner(j).start()

            @pl.when(has_down & before_seam)
            def _():
                grad_corner_direct(j).start()

        @pl.when(j >= LAG)
        def _():
            k = j - LAG
            add_down(k)

            @pl.when(has_right)
            def _():
                grad_side(k).start()

        return carry

    lax.fori_loop(0, CHUNKS + LAG, backward_step, 0)

    def unroll_term(step, carry):
        base = step * QUARTER
        rows = pl.ds(pl.multiple_of(base, QUARTER), QUARTER)
        picks = [one_hot((QUARTER, WIN), 1, base, place[2 * s]) for s in range(SLOTS)]
        pick = jnp.concatenate(picks, axis=1)
        for part in range(2):
            columns = pl.ds(part * WIN, WIN)
            probe_sum[part, rows, :] = dot(pick, term_hi[:, columns]) + dot(pick, term_lo[:, columns])
        return carry

    lax.fori_loop(0, 4, unroll_term, 0)

    half = WIN // 2
    mine = pl.multiple_of(core * half, half)
    theirs = pl.multiple_of((1 - core) * half, half)
    pair_copy = remote(
        probe_sum.at[:, pl.ds(theirs, half), :], pair_in, pair_s, pair_r, partner
    )
    pair_copy.start()
    pair_copy.wait_recv()

    def add_pair(k, carry):
        for part in range(2):
            rows = pl.ds(pl.multiple_of(mine + k * ROWS, ROWS), ROWS)
            probe_sum[part, rows, :] += pair_in[part, chunk_rows(k), :]
        return carry

    lax.fori_loop(0, half // ROWS, add_pair, 0)

    def z_copy(step):
        peer = (z + step) % 4
        rows = pl.ds(pl.multiple_of(mine + peer * ROWS, ROWS), ROWS)
        return remote(
            probe_sum.at[:, rows, :], z_in.at[step - 1], z_s.at[step - 1], z_r.at[step - 1],
            device_at(peer, y, x, core),
        )

    for step in (2, 1, 3):
        z_copy(step).start()
    z_rows = pl.ds(pl.multiple_of(mine + z * ROWS, ROWS), ROWS)
    for step in (1, 2, 3):
        z_copy(step).wait_recv()
    for part in range(2):
        probe_sum[part, z_rows, :] += z_in[0, part] + z_in[1, part] + z_in[2, part]

    def piece(index):
        return index // 8, pl.ds(pl.multiple_of(mine + z * ROWS + (index % 8) * 8, 8), 8)

    def plane_copy(step):
        peer = (plane_me + step) % 16
        part, rows = piece(peer)
        return remote(
            probe_sum.at[part, rows, :], plane_in.at[step - 1], plane_s.at[step - 1],
            plane_r.at[step - 1], device_at(z, peer // 4, peer % 4, core),
        )

    def start_plane(step, carry):
        plane_copy(step).start()
        return carry

    lax.fori_loop(1, 16, start_plane, 0)
    my_part, my_rows = piece(plane_me)

    def add_plane(step, total):
        plane_copy(step).wait_recv()
        return total + plane_in[step - 1]

    total = lax.fori_loop(1, 16, add_plane, probe_sum[my_part, my_rows, :])
    gathered[my_part, my_rows, :] = total * (1.0 / (TILES * COLS * SLOTS))

    def gather_copy(step):
        peer = (plane_me + step) % 16
        return remote(
            gathered.at[my_part, my_rows, :], gathered.at[my_part, my_rows, :],
            ag_s.at[step - 1], ag_r.at[step - 1], device_at(z, peer // 4, peer % 4, core),
        )

    def start_gather(step, carry):
        gather_copy(step).start()
        return carry

    def wait_gather(step, carry):
        gather_copy(step).wait_recv()
        return carry

    lax.fori_loop(1, 16, start_gather, 0)
    lax.fori_loop(1, 16, wait_gather, 0)

    def z_gather(step):
        peer = (z + step) % 4
        return remote(
            gathered.at[:, z_rows, :], gathered.at[:, z_rows, :], zg_s.at[step - 1],
            zg_r.at[step - 1], device_at(peer, y, x, core),
        )

    for step in (2, 1, 3):
        z_gather(step).start()
    for step in (1, 2, 3):
        z_gather(step).wait_recv()
    pair_gather = remote(
        gathered.at[:, pl.ds(mine, half), :], gathered.at[:, pl.ds(mine, half), :], pg_s, pg_r,
        partner,
    )
    pair_gather.start()

    def out_copy(k):
        rows = chunk_rows(k)
        return pltpu.make_async_copy(
            grad.at[0, :, rows, :], out_obj.at[:, rows, :], out_sem.at[k]
        )

    def finish(k, carry):
        rows = chunk_rows(k)

        @pl.when(has_left)
        def _():
            grad_side(k).wait_recv()
            for part in range(2):
                grad[0, part, rows, :] += back[RIGHT, part, rows, :]

        @pl.when(after_seam & has_up)
        def _():
            grad_corner(k).wait_recv()
            for part in range(2):
                grad[0, part, rows, :] += back[CORNER, part, rows, :]

        @pl.when(has_up)
        def _():
            grad_down(k).wait_recv()
            for part in range(2):
                grad[0, part, rows, :] += back[LOWER, part, rows, :]

        out_copy(k).start()
        return carry

    lax.fori_loop(0, CHUNKS, finish, 0)
    pair_gather.wait_recv()
    probe_out = pltpu.make_async_copy(gathered, out_probe, out_sem.at[CHUNKS])
    probe_out.start()

    def drain(k, carry):
        @pl.when(has_up)
        def _():
            up_copy(k).wait_send()

        @pl.when(has_left)
        def _():
            side_copy(k).wait_send()

        @pl.when(passes_on | (has_up & after_seam))
        def _():
            corner_copy(k).wait_send()

        @pl.when(has_right)
        def _():
            grad_side(k).wait_send()

        @pl.when(has_down)
        def _():
            grad_down(k).wait_send()

        @pl.when(has_right & has_down)
        def _():
            grad_corner(k).wait_send()

        out_copy(k).wait()
        return carry

    lax.fori_loop(0, CHUNKS, drain, 0)

    def drain_plane(step, carry):
        plane_copy(step).wait_send()
        gather_copy(step).wait_send()
        return carry

    lax.fori_loop(1, 16, drain_plane, 0)
    for step in (1, 2, 3):
        z_copy(step).wait_send()
        z_gather(step).wait_send()
    pair_copy.wait_send()
    pair_gather.wait_send()
    probe_out.wait()


def on_device(object_field, probe_field, offsets, counts, intensity):
    place = offsets.reshape(2 * SLOTS)
    count_row = counts.reshape(COLS)
    measured = intensity.reshape(SLOTS, WIN, WIN)
    row_hi, row_lo = row_tables()
    col_hi, col_lo = column_tables()
    block = (2, WIN, WIN)
    dma = pltpu.SemaphoreType.DMA
    anywhere = pl.BlockSpec(memory_space=pl.ANY)
    scalars = pl.BlockSpec(memory_space=pltpu.SMEM)
    return pl.pallas_call(
        kernel,
        name="ptycho_step",
        out_shape=(jax.ShapeDtypeStruct(block, F32), jax.ShapeDtypeStruct(block, F32)),
        in_specs=[scalars, scalars] + [anywhere] * 7,
        out_specs=(anywhere, anywhere),
        scratch_shapes=[
            pltpu.VMEM(block, F32),
            pltpu.VMEM((3,) + block, F32),
            pltpu.VMEM((4,) + block, F32),
            pltpu.VMEM((3,) + block, F32),
            pltpu.VMEM((SLOTS,) + block, F32),
            pltpu.VMEM((SLOTS,) + block, F32),
            pltpu.VMEM((SLOTS * WIN, 2 * WIN), BF16),
            pltpu.VMEM((SLOTS * WIN, 2 * WIN), BF16),
            pltpu.VMEM((SLOTS, WIN, WIN), BF16),
            pltpu.VMEM((SLOTS, WIN, WIN), BF16),
            pltpu.VMEM((4, SLOTS, WIN, QUARTER), F32),
            pltpu.VMEM((2 * WIN, WIN), BF16),
            pltpu.VMEM((2 * WIN, WIN), BF16),
            pltpu.VMEM((2, 4, 2 * QUARTER, 2 * QUARTER), BF16),
            pltpu.VMEM((2, 4, 2 * QUARTER, 2 * QUARTER), BF16),
            pltpu.VMEM((2 * SLOTS * ROWS, 2 * WIN), BF16),
            pltpu.VMEM((2 * SLOTS * ROWS, 2 * WIN), BF16),
            pltpu.VMEM(block, F32),
            pltpu.VMEM((2, WIN // 2, WIN), F32),
            pltpu.VMEM((3, 2, ROWS, WIN), F32),
            pltpu.VMEM((15, 8, WIN), F32),
            pltpu.VMEM(block, F32),
            dma((10,)), dma((CHUNKS + 1,)),
            dma((CHUNKS,)), dma((CHUNKS,)), dma((CHUNKS,)), dma((CHUNKS,)),
            dma((CHUNKS,)), dma((CHUNKS,)), dma((CHUNKS,)), dma((CHUNKS,)),
            dma((CHUNKS,)), dma((CHUNKS,)), dma((CHUNKS,)), dma((CHUNKS,)),
            dma, dma, dma((3,)), dma((3,)), dma((15,)), dma((15,)),
            dma((15,)), dma((15,)), dma((3,)), dma((3,)), dma, dma,
        ],
        compiler_params=pltpu.CompilerParams(
            collective_id=0, has_side_effects=True, vmem_limit_bytes=62 * 1024 * 1024
        ),
        cost_estimate=pl.CostEstimate(
            flops=20_000_000_000, bytes_accessed=16_000_000, transcendentals=0
        ),
    )(
        place, count_row, object_field, probe_field, measured,
        jnp.asarray(row_hi), jnp.asarray(row_lo), jnp.asarray(col_hi), jnp.asarray(col_lo),
    )


def solution(mesh):
    placed = (
        P(None, "tile", "pos"),
        P(),
        P("tile", "pos", None, None),
        P("tile", None),
        P("tile", "pos", None, None, None),
    )
    return jax.shard_map(
        on_device,
        mesh=mesh,
        in_specs=placed,
        out_specs=(P(None, "tile", "pos"), P()),
        check_vma=False,
    )
```

```python
import functools
import math

import jax
import jax.numpy as jnp
import numpy as np
from jax import lax
from jax.experimental import pallas as pl
from jax.experimental.pallas import tpu as pltpu
from jax.sharding import PartitionSpec as P

MESH = pl.DeviceIdType.MESH
WIN = 512
SLOTS = 3
ROWS = 64
CHUNKS = WIN // ROWS
LAG = 1
TILES = 8
COLS = 16
SEAM = 8
QUARTER = WIN // 4
SLAB = 256
RIGHT, LOWER, CORNER = 0, 1, 2
F32 = jnp.float32
BF16 = jnp.bfloat16


def split_table(table):
    high = table.astype(BF16)
    low = (table - high.astype(np.float64)).astype(BF16)
    return high, low


def row_tables():
    points = np.arange(WIN)
    angles = (points[:, None] * points[None, :] % WIN) * (2.0 * math.pi / WIN)
    stacked = np.concatenate([np.cos(angles), np.sin(angles)], axis=0) / math.sqrt(WIN)
    return split_table(stacked)


def column_tables():
    blocks = []
    for residue in range(4):
        freqs = 4 * np.arange(QUARTER) + residue
        angles = (freqs[:, None] * np.arange(QUARTER)[None, :] % WIN) * (2.0 * math.pi / WIN)
        cosine = np.cos(angles) / math.sqrt(WIN)
        sine = np.sin(angles) / math.sqrt(WIN)
        blocks.append(np.block([[cosine, sine], [-sine, cosine]]))
    forward = np.stack(blocks)
    backward = np.swapaxes(forward, 1, 2)
    return split_table(np.stack([forward, backward]))


def split_value(value):
    high = value.astype(BF16)
    low = (value - high.astype(F32)).astype(BF16)
    return high, low


def dot(left, right):
    return jnp.dot(left, right, preferred_element_type=F32)


def one_hot(shape, axis, base, amount):
    along = lax.broadcasted_iota(jnp.int32, shape, axis)
    other = lax.broadcasted_iota(jnp.int32, shape, 1 - axis)
    return jnp.where(along == ((other + (base + amount)) & (WIN - 1)), 1.0, 0.0).astype(BF16)


def chunk_rows(k):
    return pl.ds(pl.multiple_of(k * ROWS, ROWS), ROWS)


def device_at(z, y, x, core):
    return (z * 2 + y % 2, ((y // 2) * 4 + x) * 2 + core)


def kernel(
    place, counts, obj, probe, inten, row_hi, row_lo, col_hi, col_lo,
    out_obj, out_probe,
    own, halo, grad, back, spec, turned, term_hi, term_lo, roll_cols, unroll_cols, measured,
    wh, wl, ch, cl, left_hi, left_lo,
    probe_sum, pair_in, z_in, plane_in, gathered,
    load_sem, out_sem,
    up_s, up_r, side_s, side_r, cor_s, cor_r,
    gb_s, gb_r, gc_s, gc_r, gd_s, gd_r,
    pair_s, pair_r, z_s, z_r, plane_s, plane_r, ag_s, ag_r, zg_s, zg_r, pg_s, pg_r,
):
    t = lax.axis_index("tile")
    p = lax.axis_index("pos")
    z = t // 2
    core = p % 2
    x = (p // 2) % 4
    y = (p // 8) * 2 + t % 2
    plane_me = y * 4 + x
    own_count = counts[p]
    partner = (t, p + 1 - 2 * core)

    loads = [
        pltpu.make_async_copy(obj, own, load_sem.at[0]),
        pltpu.make_async_copy(probe, probe_sum, load_sem.at[1]),
        pltpu.make_async_copy(row_hi, wh, load_sem.at[2]),
        pltpu.make_async_copy(row_lo, wl, load_sem.at[3]),
        pltpu.make_async_copy(col_hi, ch, load_sem.at[4]),
        pltpu.make_async_copy(col_lo, cl, load_sem.at[5]),
    ]
    for lanes in range(4):
        loads.append(
            pltpu.make_async_copy(
                inten.at[:, :, pl.ds(lanes * QUARTER, QUARTER)], measured.at[lanes],
                load_sem.at[6 + lanes],
            )
        )
    for load in loads:
        load.start()

    barrier = pltpu.get_barrier_semaphore()

    def greet(device):
        pl.semaphore_signal(barrier, inc=1, device_id=device, device_id_type=MESH)

    t_up = (t + TILES - 1) % TILES
    t_down = (t + 1) % TILES
    p_left = (p + COLS - 1) % COLS
    p_right = (p + 1) % COLS
    for device in (
        (t_up, p), (t_down, p), (t, p_left), (t, p_right), (t_up, p_left), (t_down, p_right),
    ):
        greet(device)
    for step in range(1, 4):
        greet(device_at((z + step) % 4, y, x, core))

    def greet_plane(step, carry):
        peer = (plane_me + step) % 16
        greet(device_at(z, peer // 4, peer % 4, core))
        return carry

    lax.fori_loop(1, 16, greet_plane, 0)
    pl.semaphore_wait(barrier, 6 + 3 + 15)

    def remote(source, target, send, recv, device):
        return pltpu.make_async_remote_copy(
            src_ref=source, dst_ref=target, send_sem=send, recv_sem=recv,
            device_id=device, device_id_type=MESH,
        )

    def up_copy(k):
        rows = chunk_rows(k)
        return remote(
            obj.at[:, rows, :], halo.at[LOWER, :, rows, :], up_s.at[k], up_r.at[k], (t_up, p)
        )

    def side_copy(k):
        rows = chunk_rows(k)
        return remote(
            obj.at[:, rows, :], halo.at[RIGHT, :, rows, :], side_s.at[k], side_r.at[k], (t, p_left)
        )

    def corner_copy(k):
        rows = chunk_rows(k)
        return remote(
            halo.at[LOWER, :, rows, :], halo.at[CORNER, :, rows, :], cor_s.at[k], cor_r.at[k],
            (t, p_left),
        )

    def corner_direct(k):
        rows = chunk_rows(k)
        return remote(
            obj.at[:, rows, :], halo.at[CORNER, :, rows, :], cor_s.at[k], cor_r.at[k],
            (t_up, p_left),
        )

    def grad_side(k):
        rows = chunk_rows(k)
        return remote(
            grad.at[1, :, rows, :], back.at[RIGHT, :, rows, :], gb_s.at[k], gb_r.at[k],
            (t, p_right),
        )

    def grad_down(k):
        rows = chunk_rows(k)
        return remote(
            grad.at[2, :, rows, :], back.at[LOWER, :, rows, :], gc_s.at[k], gc_r.at[k],
            (t_down, p),
        )

    def grad_corner(k):
        rows = chunk_rows(k)
        return remote(
            grad.at[3, :, rows, :], back.at[CORNER, :, rows, :], gd_s.at[k], gd_r.at[k],
            (t, p_right),
        )

    def grad_corner_direct(k):
        rows = chunk_rows(k)
        return remote(
            grad.at[3, :, rows, :], back.at[CORNER, :, rows, :], gd_s.at[k], gd_r.at[k],
            (t_down, p_right),
        )

    has_up = t > 0
    has_down = t < TILES - 1
    has_left = p > 0
    has_right = p < COLS - 1
    after_seam = p == SEAM
    before_seam = p == SEAM - 1
    passes_on = has_left & has_down & jnp.logical_not(after_seam)

    def first_sends(k, carry):
        @pl.when(has_up)
        def _():
            up_copy(k).start()

        @pl.when(has_left)
        def _():
            side_copy(k).start()

        @pl.when(has_up & after_seam)
        def _():
            corner_direct(k).start()

        return carry

    lax.fori_loop(0, CHUNKS, first_sends, 0)

    for load in loads[:4]:
        load.wait()

    for part in range(2):
        high, low = split_value(probe_sum[part])
        term_hi[pl.ds(0, WIN), pl.ds(part * WIN, WIN)] = high
        term_lo[pl.ds(0, WIN), pl.ds(part * WIN, WIN)] = low

    def build_rolls(s, carry):
        amount = place[2 * s + 1]
        roll_cols[s] = one_hot((WIN, WIN), 1, 0, amount)
        unroll_cols[s] = one_hot((WIN, WIN), 0, 0, amount)
        return carry

    lax.fori_loop(0, SLOTS, build_rolls, 0)

    def roll_probe(step, carry):
        s = step // 4
        base = (step % 4) * QUARTER
        rows = pl.ds(pl.multiple_of(base, QUARTER), QUARTER)
        pick = one_hot((QUARTER, WIN), 1, base, WIN - place[2 * s])
        for part in range(2):
            columns = pl.ds(part * WIN, WIN)
            moved = dot(pick, term_hi[pl.ds(0, WIN), columns])
            moved += dot(pick, term_lo[pl.ds(0, WIN), columns])
            high, low = split_value(moved)
            turned[s, part, rows, :] = dot(high, roll_cols[s]) + dot(low, roll_cols[s])
        return carry

    lax.fori_loop(0, SLOTS * 4, roll_probe, 0)

    row_iota = lax.broadcasted_iota(jnp.int32, (ROWS, WIN), 0)
    col_iota = lax.broadcasted_iota(jnp.int32, (ROWS, WIN), 1)

    def slot_masks(s, k):
        above = (row_iota + k * ROWS) < place[2 * s]
        before = col_iota < place[2 * s + 1]
        return above, before

    def patch_part(part, rows, above, before):
        upper = jnp.where(before, halo[RIGHT, part, rows, :], own[part, rows, :])
        lower = jnp.where(before, halo[CORNER, part, rows, :], halo[LOWER, part, rows, :])
        return jnp.where(above, lower, upper)

    def put_left(s, real, imag, sign):
        top = pl.ds(s * ROWS, ROWS)
        low_rows = pl.ds((SLOTS + s) * ROWS, ROWS)
        first = pl.ds(0, WIN)
        second = pl.ds(WIN, WIN)
        for ref, re, im in zip((left_hi, left_lo), split_value(real), split_value(imag)):
            ref[top, first] = re
            ref[low_rows, first] = im
            if sign > 0:
                ref[top, second] = im
                ref[low_rows, second] = -re
            else:
                ref[top, second] = -im
                ref[low_rows, second] = re

    def row_transform(cols):
        columns = pl.ds(cols * SLAB, SLAB)
        high = left_hi[...]
        table = wh[:, columns]
        total = dot(high, table)
        total = total + dot(left_lo[...], table)
        return total + dot(high, wl[:, columns])

    def forward_chunk(k):
        rows = chunk_rows(k)
        for s in range(SLOTS):
            above, before = slot_masks(s, k)
            re = patch_part(0, rows, above, before)
            im = patch_part(1, rows, above, before)
            pr = turned[s, 0, rows, :]
            pi = turned[s, 1, rows, :]
            put_left(s, pr * re - pi * im, pr * im + pi * re, 1)
        for cols in range(WIN // SLAB):
            total = row_transform(cols)
            for s in range(SLOTS):
                for part in range(2):
                    base = (part * SLOTS + s) * ROWS
                    spec[s, part, rows, pl.ds(cols * SLAB, SLAB)] = total[base:base + ROWS]

    def forward_step(j, carry):
        @pl.when(j < CHUNKS)
        def _():
            @pl.when(has_down)
            def _():
                up_copy(j).wait_recv()

            @pl.when(passes_on)
            def _():
                corner_copy(j).start()

        @pl.when(j >= LAG)
        def _():
            k = j - LAG

            @pl.when(has_right)
            def _():
                side_copy(k).wait_recv()

            @pl.when(has_right & has_down)
            def _():
                corner_copy(k).wait_recv()

            forward_chunk(k)

        return carry

    lax.fori_loop(0, CHUNKS + LAG, forward_step, 0)

    for load in loads[4:]:
        load.wait()

    def middle(step, carry):
        s = step // (WIN // SLAB)
        slab = step % (WIN // SLAB)
        columns = pl.ds(pl.multiple_of(slab * SLAB, SLAB), SLAB)

        def quarter(part, j):
            return spec[s, part, pl.ds(j * QUARTER, QUARTER), columns]

        re = [quarter(0, j) for j in range(4)]
        im = [quarter(1, j) for j in range(4)]
        er, ei = re[0] + re[2], im[0] + im[2]
        fr, fi = re[0] - re[2], im[0] - im[2]
        gr, gi = re[1] + re[3], im[1] + im[3]
        hr, hi = re[1] - re[3], im[1] - im[3]
        mixed = [
            (er + gr, ei + gi), (fr + hi, fi - hr), (er - gr, ei - gi), (fr - hi, fi + hr),
        ]
        outs = []
        for q in range(4):
            high, low = split_value(jnp.concatenate(mixed[q], axis=0))
            total = dot(ch[0, q], high) + dot(cl[0, q], high) + dot(ch[0, q], low)
            sr, si = total[:QUARTER], total[QUARTER:]
            levels = [measured[2 * slab + n, s, pl.ds(q, QUARTER, stride=4), :] for n in range(2)]
            miss = sr * sr + si * si - jnp.concatenate(levels, axis=1)
            high, low = split_value(jnp.concatenate([miss * sr, miss * si], axis=0))
            total = dot(ch[1, q], high) + dot(cl[1, q], high) + dot(ch[1, q], low)
            outs.append((total[:QUARTER], total[QUARTER:]))
        (ar, ai), (br, bi), (cr, ci), (dr, di) = outs
        er, ei = ar + cr, ai + ci
        fr, fi = ar - cr, ai - ci
        gr, gi = br + dr, bi + di
        hr, hi = br - dr, bi - di
        results = [
            (er + gr, ei + gi), (fr - hi, fi + hr), (er - gr, ei - gi), (fr + hi, fi - hr),
        ]
        for j in range(4):
            for part in range(2):
                spec[s, part, pl.ds(j * QUARTER, QUARTER), columns] = results[j][part]
        return carry

    lax.fori_loop(0, SLOTS * (WIN // SLAB), middle, 0)

    def backward_chunk(k):
        rows = chunk_rows(k)
        for s in range(SLOTS):
            put_left(s, spec[s, 0, rows, :], spec[s, 1, rows, :], -1)
        for cols in range(WIN // SLAB):
            total = row_transform(cols)
            for s in range(SLOTS):
                for part in range(2):
                    base = (part * SLOTS + s) * ROWS
                    spec[s, part, rows, pl.ds(cols * SLAB, SLAB)] = total[base:base + ROWS]
        zero = jnp.zeros((ROWS, WIN), F32)
        sums = [[zero, zero] for _ in range(4)]
        for s in range(SLOTS):
            used = own_count > s
            above, before = slot_masks(s, k)
            br = spec[s, 0, rows, :]
            bi = spec[s, 1, rows, :]
            pr = turned[s, 0, rows, :]
            pi = turned[s, 1, rows, :]
            terms = (pr * br + pi * bi, pr * bi - pi * br)
            for part in range(2):
                term = jnp.where(used, terms[part], zero)
                lower = jnp.where(above, term, zero)
                upper = term - lower
                upper_right = jnp.where(before, upper, zero)
                lower_right = jnp.where(before, lower, zero)
                sums[0][part] += upper - upper_right
                sums[1][part] += upper_right
                sums[2][part] += lower - lower_right
                sums[3][part] += lower_right
            re = patch_part(0, rows, above, before)
            im = patch_part(1, rows, above, before)
            terms = (re * br + im * bi, re * bi - im * br)
            high, low = split_value(jnp.where(used, jnp.concatenate(terms, axis=0), 0.0))
            moved = dot(high, unroll_cols[s]) + dot(low, unroll_cols[s])
            high, low = split_value(moved)
            term_rows = pl.ds(pl.multiple_of(s * WIN + k * ROWS, ROWS), ROWS)
            for part in range(2):
                columns = pl.ds(part * WIN, WIN)
                term_hi[term_rows, columns] = high[part * ROWS:(part + 1) * ROWS]
                term_lo[term_rows, columns] = low[part * ROWS:(part + 1) * ROWS]
        for block in range(4):
            for part in range(2):
                grad[block, part, rows, :] = sums[block][part]

    receives_corner = has_left & jnp.logical_not(after_seam) & has_down

    def add_down(k):
        rows = chunk_rows(k)

        @pl.when(receives_corner)
        def _():
            grad_corner(k).wait_recv()
            for part in range(2):
                grad[2, part, rows, :] += back[CORNER, part, rows, :]

        @pl.when(has_down)
        def _():
            grad_down(k).start()

    def backward_step(j, carry):
        @pl.when(j < CHUNKS)
        def _():
            backward_chunk(j)

            @pl.when(has_right & has_down & jnp.logical_not(before_seam))
            def _():
                grad_corner(j).start()

            @pl.when(has_down & before_seam)
            def _():
                grad_corner_direct(j).start()

            @pl.when(before_seam)
            def _():
                grad_side(j).start()

        @pl.when(j >= LAG)
        def _():
            k = j - LAG
            add_down(k)

        return carry

    lax.fori_loop(0, CHUNKS + LAG, backward_step, 0)

    def send_side(k, carry):
        @pl.when(has_right & jnp.logical_not(before_seam))
        def _():
            grad_side(k).start()

        return carry

    lax.fori_loop(0, CHUNKS, send_side, 0)

    def unroll_term(step, carry):
        base = ((step // 2 + 1 - core) % 2) * (WIN // 2) + (step % 2) * QUARTER
        rows = pl.ds(pl.multiple_of(base, QUARTER), QUARTER)
        picks = [one_hot((QUARTER, WIN), 1, base, place[2 * s]) for s in range(SLOTS)]
        pick = jnp.concatenate(picks, axis=1)
        for part in range(2):
            columns = pl.ds(part * WIN, WIN)
            probe_sum[part, rows, :] = dot(pick, term_hi[:, columns]) + dot(pick, term_lo[:, columns])
        return carry

    half = WIN // 2
    mine = pl.multiple_of(core * half, half)
    theirs = pl.multiple_of((1 - core) * half, half)
    z_rows = pl.ds(pl.multiple_of(mine + z * ROWS, ROWS), ROWS)

    def pair_copy(part):
        return remote(
            probe_sum.at[part, pl.ds(theirs, half), :], pair_in.at[part], pair_s.at[part],
            pair_r.at[part], partner,
        )

    lax.fori_loop(0, 2, unroll_term, 0)
    for part in range(2):
        pair_copy(part).start()
    lax.fori_loop(2, 4, unroll_term, 0)

    def z_copy(part, step):
        peer = (z + step) % 4
        rows = pl.ds(pl.multiple_of(mine + peer * ROWS, ROWS), ROWS)
        return remote(
            probe_sum.at[part, rows, :], z_in.at[part, step - 1], z_s.at[part, step - 1],
            z_r.at[part, step - 1], device_at(peer, y, x, core),
        )

    def piece(index):
        return index // 8, pl.ds(pl.multiple_of(mine + z * ROWS + (index % 8) * 8, 8), 8)

    my_part, my_rows = piece(plane_me)

    def plane_copy(step):
        peer = (plane_me + step) % 16
        part, rows = piece(peer)
        return remote(
            probe_sum.at[part, rows, :], plane_in.at[step - 1], plane_s.at[step - 1],
            plane_r.at[step - 1], device_at(z, peer // 4, peer % 4, core),
        )

    def gather_copy(step):
        peer = (plane_me + step) % 16
        return remote(
            gathered.at[my_part, my_rows, :], gathered.at[my_part, my_rows, :],
            ag_s.at[step - 1], ag_r.at[step - 1], device_at(z, peer // 4, peer % 4, core),
        )

    def z_gather(part, step):
        peer = (z + step) % 4
        return remote(
            gathered.at[part, z_rows, :], gathered.at[part, z_rows, :], zg_s.at[part, step - 1],
            zg_r.at[part, step - 1], device_at(peer, y, x, core),
        )

    def pair_gather(part):
        rows = pl.ds(mine, half)
        return remote(
            gathered.at[part, rows, :], gathered.at[part, rows, :], pg_s.at[part], pg_r.at[part],
            partner,
        )

    for part in range(2):
        pair_copy(part).wait_recv()

        def add_pair(k, carry):
            rows = pl.ds(pl.multiple_of(mine + k * ROWS, ROWS), ROWS)
            probe_sum[part, rows, :] += pair_in[part, chunk_rows(k), :]
            return carry

        lax.fori_loop(0, half // ROWS, add_pair, 0)
        for step in (2, 1, 3):
            z_copy(part, step).start()
    for part in range(2):
        for step in (1, 2, 3):
            z_copy(part, step).wait_recv()
        probe_sum[part, z_rows, :] += z_in[part, 0] + z_in[part, 1] + z_in[part, 2]

    def start_plane(step, carry):
        plane_copy(step).start()
        return carry

    lax.fori_loop(1, 16, start_plane, 0)

    def add_plane(step, total):
        plane_copy(step).wait_recv()
        return total + plane_in[step - 1]

    total = lax.fori_loop(1, 16, add_plane, probe_sum[my_part, my_rows, :])
    gathered[my_part, my_rows, :] = total * (1.0 / (TILES * COLS * SLOTS))

    def start_gather(step, carry):
        gather_copy(step).start()
        return carry

    def wait_gather(step, carry):
        gather_copy(step).wait_recv()
        return carry

    lax.fori_loop(1, 16, start_gather, 0)
    lax.fori_loop(1, 16, wait_gather, 0)
    for part in range(2):
        for step in (2, 1, 3):
            z_gather(part, step).start()

    def out_copy(k):
        rows = chunk_rows(k)
        return pltpu.make_async_copy(
            grad.at[0, :, rows, :], out_obj.at[:, rows, :], out_sem.at[k]
        )

    def finish(k, carry):
        rows = chunk_rows(k)

        @pl.when(has_left)
        def _():
            grad_side(k).wait_recv()
            for part in range(2):
                grad[0, part, rows, :] += back[RIGHT, part, rows, :]

        @pl.when(after_seam & has_up)
        def _():
            grad_corner(k).wait_recv()
            for part in range(2):
                grad[0, part, rows, :] += back[CORNER, part, rows, :]

        @pl.when(has_up)
        def _():
            grad_down(k).wait_recv()
            for part in range(2):
                grad[0, part, rows, :] += back[LOWER, part, rows, :]

        out_copy(k).start()
        return carry

    lax.fori_loop(0, CHUNKS, finish, 0)
    for part in range(2):
        for step in (1, 2, 3):
            z_gather(part, step).wait_recv()
        pair_gather(part).start()
    for part in range(2):
        pair_gather(part).wait_recv()
    probe_out = pltpu.make_async_copy(gathered, out_probe, out_sem.at[CHUNKS])
    probe_out.start()

    def drain(k, carry):
        @pl.when(has_up)
        def _():
            up_copy(k).wait_send()

        @pl.when(has_left)
        def _():
            side_copy(k).wait_send()

        @pl.when(passes_on | (has_up & after_seam))
        def _():
            corner_copy(k).wait_send()

        @pl.when(has_right)
        def _():
            grad_side(k).wait_send()

        @pl.when(has_down)
        def _():
            grad_down(k).wait_send()

        @pl.when(has_right & has_down)
        def _():
            grad_corner(k).wait_send()

        out_copy(k).wait()
        return carry

    lax.fori_loop(0, CHUNKS, drain, 0)

    def drain_plane(step, carry):
        plane_copy(step).wait_send()
        gather_copy(step).wait_send()
        return carry

    lax.fori_loop(1, 16, drain_plane, 0)
    for part in range(2):
        for step in (1, 2, 3):
            z_copy(part, step).wait_send()
            z_gather(part, step).wait_send()
        pair_copy(part).wait_send()
        pair_gather(part).wait_send()
    probe_out.wait()


def on_device(object_field, probe_field, offsets, counts, intensity):
    place = offsets.reshape(2 * SLOTS)
    count_row = counts.reshape(COLS)
    measured = intensity.reshape(SLOTS, WIN, WIN)
    row_hi, row_lo = row_tables()
    col_hi, col_lo = column_tables()
    block = (2, WIN, WIN)
    dma = pltpu.SemaphoreType.DMA
    anywhere = pl.BlockSpec(memory_space=pl.ANY)
    scalars = pl.BlockSpec(memory_space=pltpu.SMEM)
    return pl.pallas_call(
        kernel,
        name="ptycho_step",
        out_shape=(jax.ShapeDtypeStruct(block, F32), jax.ShapeDtypeStruct(block, F32)),
        in_specs=[scalars, scalars] + [anywhere] * 7,
        out_specs=(anywhere, anywhere),
        scratch_shapes=[
            pltpu.VMEM(block, F32),
            pltpu.VMEM((3,) + block, F32),
            pltpu.VMEM((4,) + block, F32),
            pltpu.VMEM((3,) + block, F32),
            pltpu.VMEM((SLOTS,) + block, F32),
            pltpu.VMEM((SLOTS,) + block, F32),
            pltpu.VMEM((SLOTS * WIN, 2 * WIN), BF16),
            pltpu.VMEM((SLOTS * WIN, 2 * WIN), BF16),
            pltpu.VMEM((SLOTS, WIN, WIN), BF16),
            pltpu.VMEM((SLOTS, WIN, WIN), BF16),
            pltpu.VMEM((4, SLOTS, WIN, QUARTER), F32),
            pltpu.VMEM((2 * WIN, WIN), BF16),
            pltpu.VMEM((2 * WIN, WIN), BF16),
            pltpu.VMEM((2, 4, 2 * QUARTER, 2 * QUARTER), BF16),
            pltpu.VMEM((2, 4, 2 * QUARTER, 2 * QUARTER), BF16),
            pltpu.VMEM((2 * SLOTS * ROWS, 2 * WIN), BF16),
            pltpu.VMEM((2 * SLOTS * ROWS, 2 * WIN), BF16),
            pltpu.VMEM(block, F32),
            pltpu.VMEM((2, WIN // 2, WIN), F32),
            pltpu.VMEM((2, 3, ROWS, WIN), F32),
            pltpu.VMEM((15, 8, WIN), F32),
            pltpu.VMEM(block, F32),
            dma((10,)), dma((CHUNKS + 1,)),
            dma((CHUNKS,)), dma((CHUNKS,)), dma((CHUNKS,)), dma((CHUNKS,)),
            dma((CHUNKS,)), dma((CHUNKS,)), dma((CHUNKS,)), dma((CHUNKS,)),
            dma((CHUNKS,)), dma((CHUNKS,)), dma((CHUNKS,)), dma((CHUNKS,)),
            dma((2,)), dma((2,)), dma((2, 3)), dma((2, 3)), dma((15,)), dma((15,)),
            dma((15,)), dma((15,)), dma((2, 3)), dma((2, 3)), dma((2,)), dma((2,)),
        ],
        compiler_params=pltpu.CompilerParams(
            collective_id=0, has_side_effects=True, vmem_limit_bytes=62 * 1024 * 1024
        ),
        cost_estimate=pl.CostEstimate(
            flops=20_000_000_000, bytes_accessed=16_000_000, transcendentals=0
        ),
    )(
        place, count_row, object_field, probe_field, measured,
        jnp.asarray(row_hi), jnp.asarray(row_lo), jnp.asarray(col_hi), jnp.asarray(col_lo),
    )


def solution(mesh):
    placed = (
        P(None, "tile", "pos"),
        P(),
        P("tile", "pos", None, None),
        P("tile", None),
        P("tile", "pos", None, None, None),
    )
    return jax.shard_map(
        on_device,
        mesh=mesh,
        in_specs=placed,
        out_specs=(P(None, "tile", "pos"), P()),
        check_vma=False,
    )
```

```python
import functools
import math

import jax
import jax.numpy as jnp
import numpy as np
from jax import lax
from jax.experimental import pallas as pl
from jax.experimental.pallas import tpu as pltpu
from jax.sharding import PartitionSpec as P

MESH = pl.DeviceIdType.MESH
WIN = 512
SLOTS = 3
ROWS = 64
CHUNKS = WIN // ROWS
LAG = 1
TILES = 8
COLS = 16
SEAM = 8
QUARTER = WIN // 4
SLAB = 256
RIGHT, LOWER, CORNER = 0, 1, 2
F32 = jnp.float32
BF16 = jnp.bfloat16


def split_table(table):
    high = table.astype(BF16)
    low = (table - high.astype(np.float64)).astype(BF16)
    return high, low


def row_tables():
    points = np.arange(WIN)
    angles = (points[:, None] * points[None, :] % WIN) * (2.0 * math.pi / WIN)
    stacked = np.concatenate([np.cos(angles), np.sin(angles)], axis=0) / math.sqrt(WIN)
    return split_table(stacked)


def column_tables():
    blocks = []
    for residue in range(4):
        freqs = 4 * np.arange(QUARTER) + residue
        angles = (freqs[:, None] * np.arange(QUARTER)[None, :] % WIN) * (2.0 * math.pi / WIN)
        cosine = np.cos(angles) / math.sqrt(WIN)
        sine = np.sin(angles) / math.sqrt(WIN)
        blocks.append(np.block([[cosine, sine], [-sine, cosine]]))
    forward = np.stack(blocks)
    backward = np.swapaxes(forward, 1, 2)
    return split_table(np.stack([forward, backward]))


def split_value(value):
    high = value.astype(BF16)
    low = (value - high.astype(F32)).astype(BF16)
    return high, low


def dot(left, right):
    return jnp.dot(left, right, preferred_element_type=F32)


def one_hot(shape, axis, base, amount):
    along = lax.broadcasted_iota(jnp.int32, shape, axis)
    other = lax.broadcasted_iota(jnp.int32, shape, 1 - axis)
    return jnp.where(along == ((other + (base + amount)) & (WIN - 1)), 1.0, 0.0).astype(BF16)


def chunk_rows(k):
    return pl.ds(pl.multiple_of(k * ROWS, ROWS), ROWS)


def device_at(z, y, x, core):
    return (z * 2 + y % 2, ((y // 2) * 4 + x) * 2 + core)


def kernel(
    place, counts, obj, probe, inten, row_hi, row_lo, col_hi, col_lo,
    out_obj, out_probe, relay,
    own, halo, grad, back, spec, turned, term_hi, term_lo, roll_cols, unroll_cols, measured,
    wh, wl, ch, cl, left_hi, left_lo,
    probe_sum, pair_in, z_in, plane_in, gathered,
    load_sem, out_sem,
    up_s, up_r, side_s, side_r, cor_s, cor_r,
    gb_s, gb_r, gc_s, gc_r, gd_s, gd_r,
    ra_s, ra_r, rb_s, rb_r, rc_s, rc_r, rc_on, rd_s, rd_r, rd_on, pair_s, pair_r, z_s, z_r, plane_s, plane_r, ag_s, ag_r, zg_s, zg_r, pg_s, pg_r,
):
    t = lax.axis_index("tile")
    p = lax.axis_index("pos")
    z = t // 2
    core = p % 2
    x = (p // 2) % 4
    y = (p // 8) * 2 + t % 2
    plane_me = y * 4 + x
    own_count = counts[p]
    partner = (t, p + 1 - 2 * core)

    loads = [
        pltpu.make_async_copy(obj, own, load_sem.at[0]),
        pltpu.make_async_copy(probe, probe_sum, load_sem.at[1]),
        pltpu.make_async_copy(row_hi, wh, load_sem.at[2]),
        pltpu.make_async_copy(row_lo, wl, load_sem.at[3]),
        pltpu.make_async_copy(col_hi, ch, load_sem.at[4]),
        pltpu.make_async_copy(col_lo, cl, load_sem.at[5]),
    ]
    for lanes in range(4):
        loads.append(
            pltpu.make_async_copy(
                inten.at[:, :, pl.ds(lanes * QUARTER, QUARTER)], measured.at[lanes],
                load_sem.at[6 + lanes],
            )
        )
    for load in loads:
        load.start()

    barrier = pltpu.get_barrier_semaphore()

    def greet(device):
        pl.semaphore_signal(barrier, inc=1, device_id=device, device_id_type=MESH)

    t_up = (t + TILES - 1) % TILES
    t_down = (t + 1) % TILES
    t_other = t + 1 - 2 * (t % 2)
    p_left = (p + COLS - 1) % COLS
    p_right = (p + 1) % COLS
    for device in (
        (t_up, p), (t_down, p), (t, p_left), (t, p_right), (t_up, p_left), (t_down, p_right),
        (t_other, p), (t_other, p_left), (t_other, p_right),
        ((t + TILES - 2) % TILES, p_right), ((t + 2) % TILES, p_left),
        (t_down, (p + COLS - 2) % COLS), (t_up, (p + 2) % COLS),
        ((t + TILES - 2) % TILES, p), ((t + 2) % TILES, p), (t_up, p_right), (t_down, p_left),
    ):
        greet(device)
    for step in range(1, 4):
        greet(device_at((z + step) % 4, y, x, core))

    def greet_plane(step, carry):
        peer = (plane_me + step) % 16
        greet(device_at(z, peer // 4, peer % 4, core))
        return carry

    lax.fori_loop(1, 16, greet_plane, 0)
    pl.semaphore_wait(barrier, 17 + 3 + 15)

    def remote(source, target, send, recv, device):
        return pltpu.make_async_remote_copy(
            src_ref=source, dst_ref=target, send_sem=send, recv_sem=recv,
            device_id=device, device_id_type=MESH,
        )

    def up_copy(k):
        rows = chunk_rows(k)
        return remote(
            obj.at[:, rows, :], halo.at[LOWER, :, rows, :], up_s.at[k], up_r.at[k], (t_up, p)
        )

    def side_copy(k):
        rows = chunk_rows(k)
        return remote(
            obj.at[:, rows, :], halo.at[RIGHT, :, rows, :], side_s.at[k], side_r.at[k], (t, p_left)
        )

    def corner_copy(k):
        rows = chunk_rows(k)
        return remote(
            halo.at[LOWER, :, rows, :], halo.at[CORNER, :, rows, :], cor_s.at[k], cor_r.at[k],
            (t, p_left),
        )

    def corner_direct(k):
        rows = chunk_rows(k)
        return remote(
            obj.at[:, rows, :], halo.at[CORNER, :, rows, :], cor_s.at[k], cor_r.at[k],
            (t_up, p_left),
        )

    def detour(k):
        rows = chunk_rows(k)
        return remote(
            obj.at[:, rows, :], relay.at[0, :, rows, :], ra_s.at[k], ra_r.at[k], (t_other, p_left)
        )

    def detour_on(k):
        rows = chunk_rows(k)
        return remote(
            relay.at[0, :, rows, :], halo.at[RIGHT, :, rows, :], ra_s.at[k], side_r.at[k],
            (t_other, p),
        )

    def corner_detour(k):
        rows = chunk_rows(k)
        return remote(
            obj.at[:, rows, :], relay.at[1, :, rows, :], rb_s.at[k], rb_r.at[k],
            ((t + TILES - 2) % TILES, p_right),
        )

    def corner_detour_on(k):
        rows = chunk_rows(k)
        return remote(
            relay.at[1, :, rows, :], halo.at[CORNER, :, rows, :], rb_s.at[k], cor_r.at[k],
            (t_down, (p + COLS - 2) % COLS),
        )

    def grad_detour(k):
        rows = chunk_rows(k)
        return remote(
            grad.at[1, :, rows, :], relay.at[2, :, rows, :], rc_s.at[k], rc_r.at[k], (t_other, p)
        )

    def grad_detour_on(k):
        rows = chunk_rows(k)
        return remote(
            relay.at[2, :, rows, :], back.at[RIGHT, :, rows, :], rc_on.at[k], gb_r.at[k],
            (t_other, p_right),
        )

    def grad_corner_detour(k):
        rows = chunk_rows(k)
        return remote(
            grad.at[3, :, rows, :], relay.at[3, :, rows, :], rd_s.at[k], rd_r.at[k],
            ((t + 2) % TILES, p),
        )

    def grad_corner_detour_on(k):
        rows = chunk_rows(k)
        return remote(
            relay.at[3, :, rows, :], back.at[CORNER, :, rows, :], rd_on.at[k], gd_r.at[k],
            (t_up, p_right),
        )

    def grad_side(k):
        rows = chunk_rows(k)
        return remote(
            grad.at[1, :, rows, :], back.at[RIGHT, :, rows, :], gb_s.at[k], gb_r.at[k],
            (t, p_right),
        )

    def grad_down(k):
        rows = chunk_rows(k)
        return remote(
            grad.at[2, :, rows, :], back.at[LOWER, :, rows, :], gc_s.at[k], gc_r.at[k],
            (t_down, p),
        )

    def grad_corner(k):
        rows = chunk_rows(k)
        return remote(
            grad.at[3, :, rows, :], back.at[CORNER, :, rows, :], gd_s.at[k], gd_r.at[k],
            (t, p_right),
        )

    def grad_corner_direct(k):
        rows = chunk_rows(k)
        return remote(
            grad.at[3, :, rows, :], back.at[CORNER, :, rows, :], gd_s.at[k], gd_r.at[k],
            (t_down, p_right),
        )

    has_up = t > 0
    has_down = t < TILES - 1
    has_left = p > 0
    has_right = p < COLS - 1
    after_seam = p == SEAM
    before_seam = p == SEAM - 1
    even = t % 2 == 0
    turns_corner = even & has_up & after_seam
    relays_corner = even & (t < TILES - 2) & (p == SEAM + 1)

    turns_grad_corner = before_seam & has_down & jnp.logical_not(even)
    relays_grad_corner = before_seam & (t > 2) & jnp.logical_not(even)

    def on_detour(k):
        return k % 2 == 1

    passes_on = has_left & has_down & jnp.logical_not(after_seam)

    def first_sends(k, carry):
        @pl.when(has_up)
        def _():
            up_copy(k).start()

        @pl.when(has_left & jnp.logical_not(after_seam & on_detour(k)))
        def _():
            side_copy(k).start()

        @pl.when(after_seam & on_detour(k))
        def _():
            detour(k).start()

        @pl.when(has_up & after_seam & jnp.logical_not(even))
        def _():
            corner_direct(k).start()

        @pl.when(turns_corner)
        def _():
            corner_detour(k).start()

        return carry

    lax.fori_loop(0, CHUNKS, first_sends, 0)

    for load in loads[:4]:
        load.wait()

    for part in range(2):
        high, low = split_value(probe_sum[part])
        term_hi[pl.ds(0, WIN), pl.ds(part * WIN, WIN)] = high
        term_lo[pl.ds(0, WIN), pl.ds(part * WIN, WIN)] = low

    def build_rolls(s, carry):
        amount = place[2 * s + 1]
        roll_cols[s] = one_hot((WIN, WIN), 1, 0, amount)
        unroll_cols[s] = one_hot((WIN, WIN), 0, 0, amount)
        return carry

    lax.fori_loop(0, SLOTS, build_rolls, 0)

    def roll_probe(step, carry):
        s = step // 4
        base = (step % 4) * QUARTER
        rows = pl.ds(pl.multiple_of(base, QUARTER), QUARTER)
        pick = one_hot((QUARTER, WIN), 1, base, WIN - place[2 * s])
        for part in range(2):
            columns = pl.ds(part * WIN, WIN)
            moved = dot(pick, term_hi[pl.ds(0, WIN), columns])
            moved += dot(pick, term_lo[pl.ds(0, WIN), columns])
            high, low = split_value(moved)
            turned[s, part, rows, :] = dot(high, roll_cols[s]) + dot(low, roll_cols[s])
        return carry

    lax.fori_loop(0, SLOTS * 4, roll_probe, 0)

    row_iota = lax.broadcasted_iota(jnp.int32, (ROWS, WIN), 0)
    col_iota = lax.broadcasted_iota(jnp.int32, (ROWS, WIN), 1)

    def slot_masks(s, k):
        above = (row_iota + k * ROWS) < place[2 * s]
        before = col_iota < place[2 * s + 1]
        return above, before

    def patch_part(part, rows, above, before):
        upper = jnp.where(before, halo[RIGHT, part, rows, :], own[part, rows, :])
        lower = jnp.where(before, halo[CORNER, part, rows, :], halo[LOWER, part, rows, :])
        return jnp.where(above, lower, upper)

    def put_left(s, real, imag, sign):
        top = pl.ds(s * ROWS, ROWS)
        low_rows = pl.ds((SLOTS + s) * ROWS, ROWS)
        first = pl.ds(0, WIN)
        second = pl.ds(WIN, WIN)
        for ref, re, im in zip((left_hi, left_lo), split_value(real), split_value(imag)):
            ref[top, first] = re
            ref[low_rows, first] = im
            if sign > 0:
                ref[top, second] = im
                ref[low_rows, second] = -re
            else:
                ref[top, second] = -im
                ref[low_rows, second] = re

    def row_transform(cols):
        columns = pl.ds(cols * SLAB, SLAB)
        high = left_hi[...]
        table = wh[:, columns]
        total = dot(high, table)
        total = total + dot(left_lo[...], table)
        return total + dot(high, wl[:, columns])

    def forward_chunk(k):
        rows = chunk_rows(k)
        for s in range(SLOTS):
            above, before = slot_masks(s, k)
            re = patch_part(0, rows, above, before)
            im = patch_part(1, rows, above, before)
            pr = turned[s, 0, rows, :]
            pi = turned[s, 1, rows, :]
            put_left(s, pr * re - pi * im, pr * im + pi * re, 1)
        for cols in range(WIN // SLAB):
            total = row_transform(cols)
            for s in range(SLOTS):
                for part in range(2):
                    base = (part * SLOTS + s) * ROWS
                    spec[s, part, rows, pl.ds(cols * SLAB, SLAB)] = total[base:base + ROWS]

    def forward_step(j, carry):
        @pl.when(j < CHUNKS)
        def _():
            @pl.when(before_seam & on_detour(j))
            def _():
                detour(j).wait_recv()
                detour_on(j).start()

            @pl.when(relays_corner)
            def _():
                corner_detour(j).wait_recv()
                corner_detour_on(j).start()

            @pl.when(has_down)
            def _():
                up_copy(j).wait_recv()

            @pl.when(passes_on)
            def _():
                corner_copy(j).start()

        @pl.when(j >= LAG)
        def _():
            k = j - LAG

            @pl.when(has_right)
            def _():
                side_copy(k).wait_recv()

            @pl.when(has_right & has_down)
            def _():
                corner_copy(k).wait_recv()

            forward_chunk(k)

        return carry

    lax.fori_loop(0, CHUNKS + LAG, forward_step, 0)

    for load in loads[4:]:
        load.wait()

    def middle(step, carry):
        s = step // (WIN // SLAB)
        slab = step % (WIN // SLAB)
        columns = pl.ds(pl.multiple_of(slab * SLAB, SLAB), SLAB)

        def quarter(part, j):
            return spec[s, part, pl.ds(j * QUARTER, QUARTER), columns]

        re = [quarter(0, j) for j in range(4)]
        im = [quarter(1, j) for j in range(4)]
        er, ei = re[0] + re[2], im[0] + im[2]
        fr, fi = re[0] - re[2], im[0] - im[2]
        gr, gi = re[1] + re[3], im[1] + im[3]
        hr, hi = re[1] - re[3], im[1] - im[3]
        mixed = [
            (er + gr, ei + gi), (fr + hi, fi - hr), (er - gr, ei - gi), (fr - hi, fi + hr),
        ]
        outs = []
        for q in range(4):
            high, low = split_value(jnp.concatenate(mixed[q], axis=0))
            total = dot(ch[0, q], high) + dot(cl[0, q], high) + dot(ch[0, q], low)
            sr, si = total[:QUARTER], total[QUARTER:]
            levels = [measured[2 * slab + n, s, pl.ds(q, QUARTER, stride=4), :] for n in range(2)]
            miss = sr * sr + si * si - jnp.concatenate(levels, axis=1)
            high, low = split_value(jnp.concatenate([miss * sr, miss * si], axis=0))
            total = dot(ch[1, q], high) + dot(cl[1, q], high) + dot(ch[1, q], low)
            outs.append((total[:QUARTER], total[QUARTER:]))
        (ar, ai), (br, bi), (cr, ci), (dr, di) = outs
        er, ei = ar + cr, ai + ci
        fr, fi = ar - cr, ai - ci
        gr, gi = br + dr, bi + di
        hr, hi = br - dr, bi - di
        results = [
            (er + gr, ei + gi), (fr - hi, fi + hr), (er - gr, ei - gi), (fr + hi, fi - hr),
        ]
        for j in range(4):
            for part in range(2):
                spec[s, part, pl.ds(j * QUARTER, QUARTER), columns] = results[j][part]
        return carry

    lax.fori_loop(0, SLOTS * (WIN // SLAB), middle, 0)

    def backward_chunk(k):
        rows = chunk_rows(k)
        for s in range(SLOTS):
            put_left(s, spec[s, 0, rows, :], spec[s, 1, rows, :], -1)
        for cols in range(WIN // SLAB):
            total = row_transform(cols)
            for s in range(SLOTS):
                for part in range(2):
                    base = (part * SLOTS + s) * ROWS
                    spec[s, part, rows, pl.ds(cols * SLAB, SLAB)] = total[base:base + ROWS]
        zero = jnp.zeros((ROWS, WIN), F32)
        sums = [[zero, zero] for _ in range(4)]
        for s in range(SLOTS):
            used = own_count > s
            above, before = slot_masks(s, k)
            br = spec[s, 0, rows, :]
            bi = spec[s, 1, rows, :]
            pr = turned[s, 0, rows, :]
            pi = turned[s, 1, rows, :]
            terms = (pr * br + pi * bi, pr * bi - pi * br)
            for part in range(2):
                term = jnp.where(used, terms[part], zero)
                lower = jnp.where(above, term, zero)
                upper = term - lower
                upper_right = jnp.where(before, upper, zero)
                lower_right = jnp.where(before, lower, zero)
                sums[0][part] += upper - upper_right
                sums[1][part] += upper_right
                sums[2][part] += lower - lower_right
                sums[3][part] += lower_right
            re = patch_part(0, rows, above, before)
            im = patch_part(1, rows, above, before)
            terms = (re * br + im * bi, re * bi - im * br)
            high, low = split_value(jnp.where(used, jnp.concatenate(terms, axis=0), 0.0))
            moved = dot(high, unroll_cols[s]) + dot(low, unroll_cols[s])
            high, low = split_value(moved)
            term_rows = pl.ds(pl.multiple_of(s * WIN + k * ROWS, ROWS), ROWS)
            for part in range(2):
                columns = pl.ds(part * WIN, WIN)
                term_hi[term_rows, columns] = high[part * ROWS:(part + 1) * ROWS]
                term_lo[term_rows, columns] = low[part * ROWS:(part + 1) * ROWS]
        for block in range(4):
            for part in range(2):
                grad[block, part, rows, :] = sums[block][part]

    receives_corner = has_left & jnp.logical_not(after_seam) & has_down

    def add_down(k):
        rows = chunk_rows(k)

        @pl.when(receives_corner)
        def _():
            grad_corner(k).wait_recv()
            for part in range(2):
                grad[2, part, rows, :] += back[CORNER, part, rows, :]

        @pl.when(has_down)
        def _():
            grad_down(k).start()

    def backward_step(j, carry):
        @pl.when(j < CHUNKS)
        def _():
            backward_chunk(j)

            @pl.when(has_right & has_down & jnp.logical_not(before_seam))
            def _():
                grad_corner(j).start()

            @pl.when(has_down & before_seam & even)
            def _():
                grad_corner_direct(j).start()

            @pl.when(turns_grad_corner)
            def _():
                grad_corner_detour(j).start()

            @pl.when(before_seam & jnp.logical_not(on_detour(j)))
            def _():
                grad_side(j).start()

            @pl.when(before_seam & on_detour(j))
            def _():
                grad_detour(j).start()

        @pl.when(j >= LAG)
        def _():
            k = j - LAG

            add_down(k)

        return carry

    lax.fori_loop(0, CHUNKS + LAG, backward_step, 0)

    def send_side(k, carry):
        @pl.when(has_right & jnp.logical_not(before_seam))
        def _():
            grad_side(k).start()

        return carry

    lax.fori_loop(0, CHUNKS, send_side, 0)

    def unroll_term(step, carry):
        base = ((step // 2 + 1 - core) % 2) * (WIN // 2) + (step % 2) * QUARTER
        rows = pl.ds(pl.multiple_of(base, QUARTER), QUARTER)
        picks = [one_hot((QUARTER, WIN), 1, base, place[2 * s]) for s in range(SLOTS)]
        pick = jnp.concatenate(picks, axis=1)
        for part in range(2):
            columns = pl.ds(part * WIN, WIN)
            probe_sum[part, rows, :] = dot(pick, term_hi[:, columns]) + dot(pick, term_lo[:, columns])
        return carry

    half = WIN // 2
    mine = pl.multiple_of(core * half, half)
    theirs = pl.multiple_of((1 - core) * half, half)
    inner = z + 1 - 2 * (z % 2)
    outer = 3 - z
    z_peers = ((inner, outer), (outer, inner))
    z_keeps = ((((z + 1) // 2) % 2, z // 2), (z // 2, z % 2))
    z_base = []
    for first, second in z_keeps:
        z_base.append(pl.multiple_of(mine + first * QUARTER + second * ROWS, ROWS))

    def pair_copy(part):
        return remote(
            probe_sum.at[part, pl.ds(theirs, half), :], pair_in.at[part], pair_s.at[part],
            pair_r.at[part], partner,
        )

    lax.fori_loop(0, 2, unroll_term, 0)
    for part in range(2):
        pair_copy(part).start()
    lax.fori_loop(2, 4, unroll_term, 0)

    def pass_detours(k, carry):
        @pl.when(relays_grad_corner)
        def _():
            grad_corner_detour(k).wait_recv()
            grad_corner_detour_on(k).start()

        @pl.when(before_seam & on_detour(k))
        def _():
            grad_detour(k).wait_recv()
            grad_detour_on(k).start()

        return carry

    lax.fori_loop(0, CHUNKS, pass_detours, 0)

    def z_first(part):
        first = pl.multiple_of(mine + (1 - z_keeps[part][0]) * QUARTER, QUARTER)
        return remote(
            probe_sum.at[part, pl.ds(first, QUARTER), :], z_in.at[part, pl.ds(0, QUARTER), :],
            z_s.at[part, 0], z_r.at[part, 0], device_at(z_peers[part][0], y, x, core),
        )

    def z_second(part):
        keep, second = z_keeps[part]
        start = pl.multiple_of(mine + keep * QUARTER + (1 - second) * ROWS, ROWS)
        return remote(
            probe_sum.at[part, pl.ds(start, ROWS), :], z_in.at[part, pl.ds(QUARTER, ROWS), :],
            z_s.at[part, 1], z_r.at[part, 1], device_at(z_peers[part][1], y, x, core),
        )

    def z_gather_first(part):
        rows = pl.ds(z_base[part], ROWS)
        return remote(
            gathered.at[part, rows, :], gathered.at[part, rows, :], zg_s.at[part, 0],
            zg_r.at[part, 0], device_at(z_peers[part][1], y, x, core),
        )

    def z_gather_second(part):
        start = pl.multiple_of(mine + z_keeps[part][0] * QUARTER, QUARTER)
        rows = pl.ds(start, QUARTER)
        return remote(
            gathered.at[part, rows, :], gathered.at[part, rows, :], zg_s.at[part, 1],
            zg_r.at[part, 1], device_at(z_peers[part][0], y, x, core),
        )

    def piece(index):
        base = jnp.where(index // 8 == 0, z_base[0], z_base[1])
        return index // 8, pl.ds(pl.multiple_of(base + (index % 8) * 8, 8), 8)

    my_part, my_rows = piece(plane_me)

    def plane_copy(step):
        peer = (plane_me + step) % 16
        part, rows = piece(peer)
        return remote(
            probe_sum.at[part, rows, :], plane_in.at[step - 1], plane_s.at[step - 1],
            plane_r.at[step - 1], device_at(z, peer // 4, peer % 4, core),
        )

    def gather_copy(step):
        peer = (plane_me + step) % 16
        return remote(
            gathered.at[my_part, my_rows, :], gathered.at[my_part, my_rows, :],
            ag_s.at[step - 1], ag_r.at[step - 1], device_at(z, peer // 4, peer % 4, core),
        )

    def pair_gather(part):
        rows = pl.ds(mine, half)
        return remote(
            gathered.at[part, rows, :], gathered.at[part, rows, :], pg_s.at[part], pg_r.at[part],
            partner,
        )

    for part in range(2):
        pair_copy(part).wait_recv()

        def add_pair(k, carry):
            rows = pl.ds(pl.multiple_of(mine + k * ROWS, ROWS), ROWS)
            probe_sum[part, rows, :] += pair_in[part, chunk_rows(k), :]
            return carry

        lax.fori_loop(0, half // ROWS, add_pair, 0)
        z_first(part).start()
    for part in range(2):
        z_first(part).wait_recv()
        kept = pl.multiple_of(mine + z_keeps[part][0] * QUARTER, QUARTER)
        probe_sum[part, pl.ds(kept, QUARTER), :] += z_in[part, pl.ds(0, QUARTER), :]
        z_second(part).start()
    for part in range(2):
        z_second(part).wait_recv()
        probe_sum[part, pl.ds(z_base[part], ROWS), :] += z_in[part, pl.ds(QUARTER, ROWS), :]

    def start_plane(step, carry):
        plane_copy(step).start()
        return carry

    lax.fori_loop(1, 16, start_plane, 0)

    def add_plane(step, total):
        plane_copy(step).wait_recv()
        return total + plane_in[step - 1]

    total = lax.fori_loop(1, 16, add_plane, probe_sum[my_part, my_rows, :])
    gathered[my_part, my_rows, :] = total * (1.0 / (TILES * COLS * SLOTS))

    def start_gather(step, carry):
        gather_copy(step).start()
        return carry

    def wait_gather(step, carry):
        gather_copy(step).wait_recv()
        return carry

    lax.fori_loop(1, 16, start_gather, 0)
    lax.fori_loop(1, 16, wait_gather, 0)
    for part in range(2):
        z_gather_first(part).start()
    for part in range(2):
        z_gather_first(part).wait_recv()
        z_gather_second(part).start()

    def out_copy(k):
        rows = chunk_rows(k)
        return pltpu.make_async_copy(
            grad.at[0, :, rows, :], out_obj.at[:, rows, :], out_sem.at[k]
        )

    def finish(k, carry):
        rows = chunk_rows(k)

        @pl.when(has_left)
        def _():
            grad_side(k).wait_recv()
            for part in range(2):
                grad[0, part, rows, :] += back[RIGHT, part, rows, :]

        @pl.when(after_seam & has_up)
        def _():
            grad_corner(k).wait_recv()
            for part in range(2):
                grad[0, part, rows, :] += back[CORNER, part, rows, :]

        @pl.when(has_up)
        def _():
            grad_down(k).wait_recv()
            for part in range(2):
                grad[0, part, rows, :] += back[LOWER, part, rows, :]

        out_copy(k).start()
        return carry

    lax.fori_loop(0, CHUNKS, finish, 0)
    for part in range(2):
        z_gather_second(part).wait_recv()
        pair_gather(part).start()
    for part in range(2):
        pair_gather(part).wait_recv()
    probe_out = pltpu.make_async_copy(gathered, out_probe, out_sem.at[CHUNKS])
    probe_out.start()

    def drain(k, carry):
        @pl.when(has_up)
        def _():
            up_copy(k).wait_send()

        @pl.when(has_left & jnp.logical_not(after_seam & on_detour(k)))
        def _():
            side_copy(k).wait_send()

        @pl.when(after_seam & on_detour(k))
        def _():
            detour(k).wait_send()

        @pl.when(before_seam & on_detour(k))
        def _():
            detour_on(k).wait_send()

        @pl.when(passes_on | (has_up & after_seam & jnp.logical_not(even)))
        def _():
            corner_copy(k).wait_send()

        @pl.when(turns_corner)
        def _():
            corner_detour(k).wait_send()

        @pl.when(relays_corner)
        def _():
            corner_detour_on(k).wait_send()

        @pl.when(has_right & jnp.logical_not(before_seam & on_detour(k)))
        def _():
            grad_side(k).wait_send()

        @pl.when(before_seam & on_detour(k))
        def _():
            grad_detour(k).wait_send()
            grad_detour_on(k).wait_send()

        @pl.when(turns_grad_corner)
        def _():
            grad_corner_detour(k).wait_send()

        @pl.when(relays_grad_corner)
        def _():
            grad_corner_detour_on(k).wait_send()

        @pl.when(has_down)
        def _():
            grad_down(k).wait_send()

        @pl.when(has_right & has_down & jnp.logical_not(turns_grad_corner))
        def _():
            grad_corner(k).wait_send()

        out_copy(k).wait()
        return carry

    lax.fori_loop(0, CHUNKS, drain, 0)

    def drain_plane(step, carry):
        plane_copy(step).wait_send()
        gather_copy(step).wait_send()
        return carry

    lax.fori_loop(1, 16, drain_plane, 0)
    for part in range(2):
        z_first(part).wait_send()
        z_second(part).wait_send()
        z_gather_first(part).wait_send()
        z_gather_second(part).wait_send()
        pair_copy(part).wait_send()
        pair_gather(part).wait_send()
    probe_out.wait()


def on_device(object_field, probe_field, offsets, counts, intensity):
    place = offsets.reshape(2 * SLOTS)
    count_row = counts.reshape(COLS)
    measured = intensity.reshape(SLOTS, WIN, WIN)
    row_hi, row_lo = row_tables()
    col_hi, col_lo = column_tables()
    block = (2, WIN, WIN)
    dma = pltpu.SemaphoreType.DMA
    anywhere = pl.BlockSpec(memory_space=pl.ANY)
    scalars = pl.BlockSpec(memory_space=pltpu.SMEM)
    return pl.pallas_call(
        kernel,
        name="ptycho_step",
        out_shape=(
            jax.ShapeDtypeStruct(block, F32), jax.ShapeDtypeStruct(block, F32),
            jax.ShapeDtypeStruct((4,) + block, F32),
        ),
        in_specs=[scalars, scalars] + [anywhere] * 7,
        out_specs=(anywhere, anywhere, anywhere),
        scratch_shapes=[
            pltpu.VMEM(block, F32),
            pltpu.VMEM((3,) + block, F32),
            pltpu.VMEM((4,) + block, F32),
            pltpu.VMEM((3,) + block, F32),
            pltpu.VMEM((SLOTS,) + block, F32),
            pltpu.VMEM((SLOTS,) + block, F32),
            pltpu.VMEM((SLOTS * WIN, 2 * WIN), BF16),
            pltpu.VMEM((SLOTS * WIN, 2 * WIN), BF16),
            pltpu.VMEM((SLOTS, WIN, WIN), BF16),
            pltpu.VMEM((SLOTS, WIN, WIN), BF16),
            pltpu.VMEM((4, SLOTS, WIN, QUARTER), F32),
            pltpu.VMEM((2 * WIN, WIN), BF16),
            pltpu.VMEM((2 * WIN, WIN), BF16),
            pltpu.VMEM((2, 4, 2 * QUARTER, 2 * QUARTER), BF16),
            pltpu.VMEM((2, 4, 2 * QUARTER, 2 * QUARTER), BF16),
            pltpu.VMEM((2 * SLOTS * ROWS, 2 * WIN), BF16),
            pltpu.VMEM((2 * SLOTS * ROWS, 2 * WIN), BF16),
            pltpu.VMEM(block, F32),
            pltpu.VMEM((2, WIN // 2, WIN), F32),
            pltpu.VMEM((2, QUARTER + ROWS, WIN), F32),
            pltpu.VMEM((15, 8, WIN), F32),
            pltpu.VMEM(block, F32),
            dma((10,)), dma((CHUNKS + 1,)),
            dma((CHUNKS,)), dma((CHUNKS,)), dma((CHUNKS,)), dma((CHUNKS,)),
            dma((CHUNKS,)), dma((CHUNKS,)), dma((CHUNKS,)), dma((CHUNKS,)),
            dma((CHUNKS,)), dma((CHUNKS,)), dma((CHUNKS,)), dma((CHUNKS,)),
            dma((CHUNKS,)), dma((CHUNKS,)), dma((CHUNKS,)), dma((CHUNKS,)),
            dma((CHUNKS,)), dma((CHUNKS,)), dma((CHUNKS,)),
            dma((CHUNKS,)), dma((CHUNKS,)), dma((CHUNKS,)),
            dma((2,)), dma((2,)), dma((2, 2)), dma((2, 2)), dma((15,)), dma((15,)),
            dma((15,)), dma((15,)), dma((2, 2)), dma((2, 2)), dma((2,)), dma((2,)),
        ],
        compiler_params=pltpu.CompilerParams(
            collective_id=0, has_side_effects=True, vmem_limit_bytes=62 * 1024 * 1024
        ),
        cost_estimate=pl.CostEstimate(
            flops=20_000_000_000, bytes_accessed=16_000_000, transcendentals=0
        ),
    )(
        place, count_row, object_field, probe_field, measured,
        jnp.asarray(row_hi), jnp.asarray(row_lo), jnp.asarray(col_hi), jnp.asarray(col_lo),
    )[:2]


def solution(mesh):
    placed = (
        P(None, "tile", "pos"),
        P(),
        P("tile", "pos", None, None),
        P("tile", None),
        P("tile", "pos", None, None, None),
    )
    return jax.shard_map(
        on_device,
        mesh=mesh,
        in_specs=placed,
        out_specs=(P(None, "tile", "pos"), P()),
        check_vma=False,
    )
```

```python
import functools
import math

import jax
import jax.numpy as jnp
import numpy as np
from jax import lax
from jax.experimental import pallas as pl
from jax.experimental.pallas import tpu as pltpu
from jax.sharding import PartitionSpec as P

MESH = pl.DeviceIdType.MESH
WIN = 512
SLOTS = 3
ROWS = 64
CHUNKS = WIN // ROWS
LAG = 1
TILES = 8
COLS = 16
SEAM = 8
QUARTER = WIN // 4
SLAB = 256
RIGHT, LOWER, CORNER = 0, 1, 2
F32 = jnp.float32
BF16 = jnp.bfloat16


def split_table(table):
    high = table.astype(BF16)
    low = (table - high.astype(np.float64)).astype(BF16)
    return high, low


def row_tables():
    points = np.arange(WIN)
    angles = (points[:, None] * points[None, :] % WIN) * (2.0 * math.pi / WIN)
    stacked = np.concatenate([np.cos(angles), np.sin(angles)], axis=0) / math.sqrt(WIN)
    return split_table(stacked)


def column_tables():
    blocks = []
    for residue in range(4):
        freqs = 4 * np.arange(QUARTER) + residue
        angles = (freqs[:, None] * np.arange(QUARTER)[None, :] % WIN) * (2.0 * math.pi / WIN)
        cosine = np.cos(angles) / math.sqrt(WIN)
        sine = np.sin(angles) / math.sqrt(WIN)
        blocks.append(np.block([[cosine, sine], [-sine, cosine]]))
    forward = np.stack(blocks)
    backward = np.swapaxes(forward, 1, 2)
    return split_table(np.stack([forward, backward]))


def split_value(value):
    high = value.astype(BF16)
    low = (value - high.astype(F32)).astype(BF16)
    return high, low


def dot(left, right):
    return jnp.dot(left, right, preferred_element_type=F32)


def one_hot(shape, axis, base, amount):
    along = lax.broadcasted_iota(jnp.int32, shape, axis)
    other = lax.broadcasted_iota(jnp.int32, shape, 1 - axis)
    return jnp.where(along == ((other + (base + amount)) & (WIN - 1)), 1.0, 0.0).astype(BF16)


def chunk_rows(k):
    return pl.ds(pl.multiple_of(k * ROWS, ROWS), ROWS)


def device_at(z, y, x, core):
    return (z * 2 + y % 2, ((y // 2) * 4 + x) * 2 + core)


def kernel(
    place, counts, obj, probe, inten, row_hi, row_lo, col_hi, col_lo,
    out_obj, out_probe, relay,
    own, halo, grad, back, spec, turned, term_hi, term_lo, roll_cols, unroll_cols, measured,
    wh, wl, ch, cl, left_hi, left_lo,
    probe_sum, pair_in, z_in, plane_in, gathered,
    load_sem, out_sem,
    up_s, up_r, side_s, side_r, cor_s, cor_r,
    gb_s, gb_r, gc_s, gc_r, gd_s, gd_r,
    ra_s, ra_r, rb_s, rb_r, rc_s, rc_r, rc_on, rd_s, rd_r, rd_on, pair_s, pair_r, z_s, z_r, plane_s, plane_r, ag_s, ag_r, zg_s, zg_r, pg_s, pg_r,
):
    t = lax.axis_index("tile")
    p = lax.axis_index("pos")
    z = t // 2
    core = p % 2
    x = (p // 2) % 4
    y = (p // 8) * 2 + t % 2
    plane_me = y * 4 + x
    own_count = counts[p]
    partner = (t, p + 1 - 2 * core)

    loads = [
        pltpu.make_async_copy(obj, own, load_sem.at[0]),
        pltpu.make_async_copy(probe, probe_sum, load_sem.at[1]),
        pltpu.make_async_copy(row_hi, wh, load_sem.at[2]),
        pltpu.make_async_copy(row_lo, wl, load_sem.at[3]),
        pltpu.make_async_copy(col_hi, ch, load_sem.at[4]),
        pltpu.make_async_copy(col_lo, cl, load_sem.at[5]),
    ]
    for lanes in range(4):
        loads.append(
            pltpu.make_async_copy(
                inten.at[:, :, pl.ds(lanes * QUARTER, QUARTER)], measured.at[lanes],
                load_sem.at[6 + lanes],
            )
        )
    for load in loads:
        load.start()

    barrier = pltpu.get_barrier_semaphore()

    def greet(device):
        pl.semaphore_signal(barrier, inc=1, device_id=device, device_id_type=MESH)

    t_up = (t + TILES - 1) % TILES
    t_down = (t + 1) % TILES
    t_other = t + 1 - 2 * (t % 2)
    p_left = (p + COLS - 1) % COLS
    p_right = (p + 1) % COLS
    for device in (
        (t_up, p), (t_down, p), (t, p_left), (t, p_right), (t_up, p_left), (t_down, p_right),
        (t_other, p), (t_other, p_left), (t_other, p_right),
        ((t + TILES - 2) % TILES, p_right), ((t + 2) % TILES, p_left),
        (t_down, (p + COLS - 2) % COLS), (t_up, (p + 2) % COLS),
        ((t + TILES - 2) % TILES, p), ((t + 2) % TILES, p), (t_up, p_right), (t_down, p_left),
    ):
        greet(device)
    for step in range(1, 4):
        greet(device_at((z + step) % 4, y, x, core))

    def greet_plane(step, carry):
        peer = (plane_me + step) % 16
        greet(device_at(z, peer // 4, peer % 4, core))
        return carry

    lax.fori_loop(1, 16, greet_plane, 0)
    pl.semaphore_wait(barrier, 17 + 3 + 15)

    def remote(source, target, send, recv, device):
        return pltpu.make_async_remote_copy(
            src_ref=source, dst_ref=target, send_sem=send, recv_sem=recv,
            device_id=device, device_id_type=MESH,
        )

    def up_copy(k):
        rows = chunk_rows(k)
        return remote(
            obj.at[:, rows, :], halo.at[LOWER, :, rows, :], up_s.at[k], up_r.at[k], (t_up, p)
        )

    def side_copy(k):
        rows = chunk_rows(k)
        return remote(
            obj.at[:, rows, :], halo.at[RIGHT, :, rows, :], side_s.at[k], side_r.at[k], (t, p_left)
        )

    def corner_copy(k):
        rows = chunk_rows(k)
        return remote(
            halo.at[LOWER, :, rows, :], halo.at[CORNER, :, rows, :], cor_s.at[k], cor_r.at[k],
            (t, p_left),
        )

    def corner_direct(k):
        rows = chunk_rows(k)
        return remote(
            obj.at[:, rows, :], halo.at[CORNER, :, rows, :], cor_s.at[k], cor_r.at[k],
            (t_up, p_left),
        )

    def detour(k):
        rows = chunk_rows(k)
        return remote(
            obj.at[:, rows, :], relay.at[0, :, rows, :], ra_s.at[k], ra_r.at[k], (t_other, p_left)
        )

    def detour_on(k):
        rows = chunk_rows(k)
        return remote(
            relay.at[0, :, rows, :], halo.at[RIGHT, :, rows, :], ra_s.at[k], side_r.at[k],
            (t_other, p),
        )

    def corner_detour(k):
        rows = chunk_rows(k)
        return remote(
            obj.at[:, rows, :], relay.at[1, :, rows, :], rb_s.at[k], rb_r.at[k],
            ((t + TILES - 2) % TILES, p_right),
        )

    def corner_detour_on(k):
        rows = chunk_rows(k)
        return remote(
            relay.at[1, :, rows, :], halo.at[CORNER, :, rows, :], rb_s.at[k], cor_r.at[k],
            (t_down, (p + COLS - 2) % COLS),
        )

    def grad_detour(k):
        rows = chunk_rows(k)
        return remote(
            grad.at[1, :, rows, :], relay.at[2, :, rows, :], rc_s.at[k], rc_r.at[k], (t_other, p)
        )

    def grad_detour_on(k):
        rows = chunk_rows(k)
        return remote(
            relay.at[2, :, rows, :], back.at[RIGHT, :, rows, :], rc_on.at[k], gb_r.at[k],
            (t_other, p_right),
        )

    def grad_corner_detour(k):
        rows = chunk_rows(k)
        return remote(
            grad.at[3, :, rows, :], relay.at[3, :, rows, :], rd_s.at[k], rd_r.at[k],
            ((t + 2) % TILES, p),
        )

    def grad_corner_detour_on(k):
        rows = chunk_rows(k)
        return remote(
            relay.at[3, :, rows, :], back.at[CORNER, :, rows, :], rd_on.at[k], gd_r.at[k],
            (t_up, p_right),
        )

    def grad_side(k):
        rows = chunk_rows(k)
        return remote(
            grad.at[1, :, rows, :], back.at[RIGHT, :, rows, :], gb_s.at[k], gb_r.at[k],
            (t, p_right),
        )

    def grad_down(k):
        rows = chunk_rows(k)
        return remote(
            grad.at[2, :, rows, :], back.at[LOWER, :, rows, :], gc_s.at[k], gc_r.at[k],
            (t_down, p),
        )

    def grad_corner(k):
        rows = chunk_rows(k)
        return remote(
            grad.at[3, :, rows, :], back.at[CORNER, :, rows, :], gd_s.at[k], gd_r.at[k],
            (t, p_right),
        )

    def grad_corner_direct(k):
        rows = chunk_rows(k)
        return remote(
            grad.at[3, :, rows, :], back.at[CORNER, :, rows, :], gd_s.at[k], gd_r.at[k],
            (t_down, p_right),
        )

    has_up = t > 0
    has_down = t < TILES - 1
    has_left = p > 0
    has_right = p < COLS - 1
    after_seam = p == SEAM
    before_seam = p == SEAM - 1
    even = t % 2 == 0
    turns_corner = even & has_up & after_seam
    relays_corner = even & (t < TILES - 2) & (p == SEAM + 1)

    turns_grad_corner = before_seam & has_down & jnp.logical_not(even)
    relays_grad_corner = before_seam & (t > 2) & jnp.logical_not(even)

    def on_detour(k):
        return k % 2 == 1

    passes_on = has_left & has_down & jnp.logical_not(after_seam)

    def first_sends(k, carry):
        @pl.when(has_up)
        def _():
            up_copy(k).start()

        @pl.when(has_left & jnp.logical_not(after_seam & on_detour(k)))
        def _():
            side_copy(k).start()

        @pl.when(after_seam & on_detour(k))
        def _():
            detour(k).start()

        @pl.when(has_up & after_seam & jnp.logical_not(even))
        def _():
            corner_direct(k).start()

        @pl.when(turns_corner)
        def _():
            corner_detour(k).start()

        return carry

    lax.fori_loop(0, CHUNKS, first_sends, 0)

    for load in loads[:4]:
        load.wait()

    for part in range(2):
        high, low = split_value(probe_sum[part])
        term_hi[pl.ds(0, WIN), pl.ds(part * WIN, WIN)] = high
        term_lo[pl.ds(0, WIN), pl.ds(part * WIN, WIN)] = low

    def build_rolls(s, carry):
        amount = place[2 * s + 1]
        roll_cols[s] = one_hot((WIN, WIN), 1, 0, amount)
        unroll_cols[s] = one_hot((WIN, WIN), 0, 0, amount)
        return carry

    lax.fori_loop(0, SLOTS, build_rolls, 0)

    def roll_probe(step, carry):
        s = step // 4
        base = (step % 4) * QUARTER
        rows = pl.ds(pl.multiple_of(base, QUARTER), QUARTER)
        pick = one_hot((QUARTER, WIN), 1, base, WIN - place[2 * s])
        for part in range(2):
            columns = pl.ds(part * WIN, WIN)
            moved = dot(pick, term_hi[pl.ds(0, WIN), columns])
            moved += dot(pick, term_lo[pl.ds(0, WIN), columns])
            high, low = split_value(moved)
            turned[s, part, rows, :] = dot(high, roll_cols[s]) + dot(low, roll_cols[s])
        return carry

    lax.fori_loop(0, SLOTS * 4, roll_probe, 0)

    row_iota = lax.broadcasted_iota(jnp.int32, (ROWS, WIN), 0)
    col_iota = lax.broadcasted_iota(jnp.int32, (ROWS, WIN), 1)

    def slot_masks(s, k):
        above = (row_iota + k * ROWS) < place[2 * s]
        before = col_iota < place[2 * s + 1]
        return above, before

    def patch_part(part, rows, above, before):
        upper = jnp.where(before, halo[RIGHT, part, rows, :], own[part, rows, :])
        lower = jnp.where(before, halo[CORNER, part, rows, :], halo[LOWER, part, rows, :])
        return jnp.where(above, lower, upper)

    def put_left(s, real, imag, sign):
        top = pl.ds(s * ROWS, ROWS)
        low_rows = pl.ds((SLOTS + s) * ROWS, ROWS)
        first = pl.ds(0, WIN)
        second = pl.ds(WIN, WIN)
        for ref, re, im in zip((left_hi, left_lo), split_value(real), split_value(imag)):
            ref[top, first] = re
            ref[low_rows, first] = im
            if sign > 0:
                ref[top, second] = im
                ref[low_rows, second] = -re
            else:
                ref[top, second] = -im
                ref[low_rows, second] = re

    def row_transform(cols):
        columns = pl.ds(cols * SLAB, SLAB)
        high = left_hi[...]
        table = wh[:, columns]
        total = dot(high, table)
        total = total + dot(left_lo[...], table)
        return total + dot(high, wl[:, columns])

    def forward_chunk(k):
        rows = chunk_rows(k)
        for s in range(SLOTS):
            above, before = slot_masks(s, k)
            re = patch_part(0, rows, above, before)
            im = patch_part(1, rows, above, before)
            pr = turned[s, 0, rows, :]
            pi = turned[s, 1, rows, :]
            put_left(s, pr * re - pi * im, pr * im + pi * re, 1)
        for cols in range(WIN // SLAB):
            total = row_transform(cols)
            for s in range(SLOTS):
                for part in range(2):
                    base = (part * SLOTS + s) * ROWS
                    spec[s, part, rows, pl.ds(cols * SLAB, SLAB)] = total[base:base + ROWS]

    def forward_step(j, carry):
        @pl.when(j < CHUNKS)
        def _():
            @pl.when(before_seam & on_detour(j))
            def _():
                detour(j).wait_recv()
                detour_on(j).start()

            @pl.when(relays_corner)
            def _():
                corner_detour(j).wait_recv()
                corner_detour_on(j).start()

            @pl.when(has_down)
            def _():
                up_copy(j).wait_recv()

            @pl.when(passes_on)
            def _():
                corner_copy(j).start()

        @pl.when(j >= LAG)
        def _():
            k = j - LAG

            @pl.when(has_right)
            def _():
                side_copy(k).wait_recv()

            @pl.when(has_right & has_down)
            def _():
                corner_copy(k).wait_recv()

            forward_chunk(k)

        return carry

    lax.fori_loop(0, CHUNKS + LAG, forward_step, 0)

    for load in loads[4:]:
        load.wait()

    def middle(step, carry):
        s = step // (WIN // SLAB)
        slab = step % (WIN // SLAB)
        columns = pl.ds(pl.multiple_of(slab * SLAB, SLAB), SLAB)

        def quarter(part, j):
            return spec[s, part, pl.ds(j * QUARTER, QUARTER), columns]

        re = [quarter(0, j) for j in range(4)]
        im = [quarter(1, j) for j in range(4)]
        er, ei = re[0] + re[2], im[0] + im[2]
        fr, fi = re[0] - re[2], im[0] - im[2]
        gr, gi = re[1] + re[3], im[1] + im[3]
        hr, hi = re[1] - re[3], im[1] - im[3]
        mixed = [
            (er + gr, ei + gi), (fr + hi, fi - hr), (er - gr, ei - gi), (fr - hi, fi + hr),
        ]
        outs = []
        for q in range(4):
            high, low = split_value(jnp.concatenate(mixed[q], axis=0))
            total = dot(ch[0, q], high) + dot(cl[0, q], high) + dot(ch[0, q], low)
            sr, si = total[:QUARTER], total[QUARTER:]
            levels = [measured[2 * slab + n, s, pl.ds(q, QUARTER, stride=4), :] for n in range(2)]
            miss = sr * sr + si * si - jnp.concatenate(levels, axis=1)
            high, low = split_value(jnp.concatenate([miss * sr, miss * si], axis=0))
            total = dot(ch[1, q], high) + dot(cl[1, q], high) + dot(ch[1, q], low)
            outs.append((total[:QUARTER], total[QUARTER:]))
        (ar, ai), (br, bi), (cr, ci), (dr, di) = outs
        er, ei = ar + cr, ai + ci
        fr, fi = ar - cr, ai - ci
        gr, gi = br + dr, bi + di
        hr, hi = br - dr, bi - di
        results = [
            (er + gr, ei + gi), (fr - hi, fi + hr), (er - gr, ei - gi), (fr + hi, fi - hr),
        ]
        for j in range(4):
            for part in range(2):
                spec[s, part, pl.ds(j * QUARTER, QUARTER), columns] = results[j][part]
        return carry

    lax.fori_loop(0, SLOTS * (WIN // SLAB), middle, 0)

    def backward_chunk(k):
        rows = chunk_rows(k)
        for s in range(SLOTS):
            put_left(s, spec[s, 0, rows, :], spec[s, 1, rows, :], -1)
        for cols in range(WIN // SLAB):
            total = row_transform(cols)
            for s in range(SLOTS):
                for part in range(2):
                    base = (part * SLOTS + s) * ROWS
                    spec[s, part, rows, pl.ds(cols * SLAB, SLAB)] = total[base:base + ROWS]
        zero = jnp.zeros((ROWS, WIN), F32)
        sums = [[zero, zero] for _ in range(4)]
        for s in range(SLOTS):
            used = own_count > s
            above, before = slot_masks(s, k)
            br = spec[s, 0, rows, :]
            bi = spec[s, 1, rows, :]
            pr = turned[s, 0, rows, :]
            pi = turned[s, 1, rows, :]
            terms = (pr * br + pi * bi, pr * bi - pi * br)
            for part in range(2):
                term = jnp.where(used, terms[part], zero)
                lower = jnp.where(above, term, zero)
                upper = term - lower
                upper_right = jnp.where(before, upper, zero)
                lower_right = jnp.where(before, lower, zero)
                sums[0][part] += upper - upper_right
                sums[1][part] += upper_right
                sums[2][part] += lower - lower_right
                sums[3][part] += lower_right
            re = patch_part(0, rows, above, before)
            im = patch_part(1, rows, above, before)
            terms = (re * br + im * bi, re * bi - im * br)
            high, low = split_value(jnp.where(used, jnp.concatenate(terms, axis=0), 0.0))
            moved = dot(high, unroll_cols[s]) + dot(low, unroll_cols[s])
            high, low = split_value(moved)
            term_rows = pl.ds(pl.multiple_of(s * WIN + k * ROWS, ROWS), ROWS)
            for part in range(2):
                columns = pl.ds(part * WIN, WIN)
                term_hi[term_rows, columns] = high[part * ROWS:(part + 1) * ROWS]
                term_lo[term_rows, columns] = low[part * ROWS:(part + 1) * ROWS]
        for block in range(4):
            for part in range(2):
                grad[block, part, rows, :] = sums[block][part]

    receives_corner = has_left & jnp.logical_not(after_seam) & has_down

    def add_down(k):
        rows = chunk_rows(k)

        @pl.when(receives_corner)
        def _():
            grad_corner(k).wait_recv()
            for part in range(2):
                grad[2, part, rows, :] += back[CORNER, part, rows, :]

        @pl.when(has_down)
        def _():
            grad_down(k).start()

    def backward_step(j, carry):
        @pl.when(j < CHUNKS)
        def _():
            backward_chunk(j)

            @pl.when(has_right & has_down & jnp.logical_not(before_seam))
            def _():
                grad_corner(j).start()

            @pl.when(has_down & before_seam & even)
            def _():
                grad_corner_direct(j).start()

            @pl.when(turns_grad_corner)
            def _():
                grad_corner_detour(j).start()

            @pl.when(has_right & jnp.logical_not(before_seam & on_detour(j)))
            def _():
                grad_side(j).start()

            @pl.when(before_seam & on_detour(j))
            def _():
                grad_detour(j).start()

        @pl.when(j >= LAG)
        def _():
            k = j - LAG

            add_down(k)

        return carry

    lax.fori_loop(0, CHUNKS + LAG, backward_step, 0)

    def unroll_term(step, carry):
        base = ((step // 2 + 1 - core) % 2) * (WIN // 2) + (step % 2) * QUARTER
        rows = pl.ds(pl.multiple_of(base, QUARTER), QUARTER)
        picks = [one_hot((QUARTER, WIN), 1, base, place[2 * s]) for s in range(SLOTS)]
        pick = jnp.concatenate(picks, axis=1)
        for part in range(2):
            columns = pl.ds(part * WIN, WIN)
            probe_sum[part, rows, :] = dot(pick, term_hi[:, columns]) + dot(pick, term_lo[:, columns])
        return carry

    half = WIN // 2
    mine = pl.multiple_of(core * half, half)
    theirs = pl.multiple_of((1 - core) * half, half)
    inner = z + 1 - 2 * (z % 2)
    outer = 3 - z
    z_peers = ((inner, outer), (outer, inner))
    z_keeps = ((((z + 1) // 2) % 2, z // 2), (z // 2, z % 2))
    z_base = []
    for first, second in z_keeps:
        z_base.append(pl.multiple_of(mine + first * QUARTER + second * ROWS, ROWS))

    def pair_copy(part):
        return remote(
            probe_sum.at[part, pl.ds(theirs, half), :], pair_in.at[part], pair_s.at[part],
            pair_r.at[part], partner,
        )

    lax.fori_loop(0, 2, unroll_term, 0)
    for part in range(2):
        pair_copy(part).start()
    lax.fori_loop(2, 4, unroll_term, 0)

    def pass_detours(k, carry):
        @pl.when(relays_grad_corner)
        def _():
            grad_corner_detour(k).wait_recv()
            grad_corner_detour_on(k).start()

        @pl.when(before_seam & on_detour(k))
        def _():
            grad_detour(k).wait_recv()
            grad_detour_on(k).start()

        return carry

    lax.fori_loop(0, CHUNKS, pass_detours, 0)

    def z_first(part):
        first = pl.multiple_of(mine + (1 - z_keeps[part][0]) * QUARTER, QUARTER)
        return remote(
            probe_sum.at[part, pl.ds(first, QUARTER), :], z_in.at[part, pl.ds(0, QUARTER), :],
            z_s.at[part, 0], z_r.at[part, 0], device_at(z_peers[part][0], y, x, core),
        )

    def z_second(part):
        keep, second = z_keeps[part]
        start = pl.multiple_of(mine + keep * QUARTER + (1 - second) * ROWS, ROWS)
        return remote(
            probe_sum.at[part, pl.ds(start, ROWS), :], z_in.at[part, pl.ds(QUARTER, ROWS), :],
            z_s.at[part, 1], z_r.at[part, 1], device_at(z_peers[part][1], y, x, core),
        )

    def z_gather_first(part):
        rows = pl.ds(z_base[part], ROWS)
        return remote(
            gathered.at[part, rows, :], gathered.at[part, rows, :], zg_s.at[part, 0],
            zg_r.at[part, 0], device_at(z_peers[part][1], y, x, core),
        )

    def z_gather_second(part):
        start = pl.multiple_of(mine + z_keeps[part][0] * QUARTER, QUARTER)
        rows = pl.ds(start, QUARTER)
        return remote(
            gathered.at[part, rows, :], gathered.at[part, rows, :], zg_s.at[part, 1],
            zg_r.at[part, 1], device_at(z_peers[part][0], y, x, core),
        )

    def piece(index):
        base = jnp.where(index // 8 == 0, z_base[0], z_base[1])
        return index // 8, pl.ds(pl.multiple_of(base + (index % 8) * 8, 8), 8)

    my_part, my_rows = piece(plane_me)

    def plane_copy(step):
        peer = (plane_me + step) % 16
        part, rows = piece(peer)
        return remote(
            probe_sum.at[part, rows, :], plane_in.at[step - 1], plane_s.at[step - 1],
            plane_r.at[step - 1], device_at(z, peer // 4, peer % 4, core),
        )

    def gather_copy(step):
        peer = (plane_me + step) % 16
        return remote(
            gathered.at[my_part, my_rows, :], gathered.at[my_part, my_rows, :],
            ag_s.at[step - 1], ag_r.at[step - 1], device_at(z, peer // 4, peer % 4, core),
        )

    def pair_gather(part):
        rows = pl.ds(mine, half)
        return remote(
            gathered.at[part, rows, :], gathered.at[part, rows, :], pg_s.at[part], pg_r.at[part],
            partner,
        )

    for part in range(2):
        pair_copy(part).wait_recv()

        def add_pair(k, carry):
            rows = pl.ds(pl.multiple_of(mine + k * ROWS, ROWS), ROWS)
            probe_sum[part, rows, :] += pair_in[part, chunk_rows(k), :]
            return carry

        lax.fori_loop(0, half // ROWS, add_pair, 0)
        z_first(part).start()
    for part in range(2):
        z_first(part).wait_recv()
        kept = pl.multiple_of(mine + z_keeps[part][0] * QUARTER, QUARTER)
        probe_sum[part, pl.ds(kept, QUARTER), :] += z_in[part, pl.ds(0, QUARTER), :]
        z_second(part).start()
    for part in range(2):
        z_second(part).wait_recv()
        probe_sum[part, pl.ds(z_base[part], ROWS), :] += z_in[part, pl.ds(QUARTER, ROWS), :]

    def start_plane(step, carry):
        plane_copy(step).start()
        return carry

    lax.fori_loop(1, 16, start_plane, 0)

    def add_plane(step, total):
        plane_copy(step).wait_recv()
        return total + plane_in[step - 1]

    total = lax.fori_loop(1, 16, add_plane, probe_sum[my_part, my_rows, :])
    gathered[my_part, my_rows, :] = total * (1.0 / (TILES * COLS * SLOTS))

    def start_gather(step, carry):
        gather_copy(step).start()
        return carry

    def wait_gather(step, carry):
        gather_copy(step).wait_recv()
        return carry

    lax.fori_loop(1, 16, start_gather, 0)
    lax.fori_loop(1, 16, wait_gather, 0)
    for part in range(2):
        z_gather_first(part).start()
    for part in range(2):
        z_gather_first(part).wait_recv()
        z_gather_second(part).start()

    def out_copy(k):
        rows = chunk_rows(k)
        return pltpu.make_async_copy(
            grad.at[0, :, rows, :], out_obj.at[:, rows, :], out_sem.at[k]
        )

    def finish(k, carry):
        rows = chunk_rows(k)

        @pl.when(has_left)
        def _():
            grad_side(k).wait_recv()
            for part in range(2):
                grad[0, part, rows, :] += back[RIGHT, part, rows, :]

        @pl.when(after_seam & has_up)
        def _():
            grad_corner(k).wait_recv()
            for part in range(2):
                grad[0, part, rows, :] += back[CORNER, part, rows, :]

        @pl.when(has_up)
        def _():
            grad_down(k).wait_recv()
            for part in range(2):
                grad[0, part, rows, :] += back[LOWER, part, rows, :]

        out_copy(k).start()
        return carry

    lax.fori_loop(0, CHUNKS, finish, 0)
    for part in range(2):
        z_gather_second(part).wait_recv()
        pair_gather(part).start()
    for part in range(2):
        pair_gather(part).wait_recv()
    probe_out = pltpu.make_async_copy(gathered, out_probe, out_sem.at[CHUNKS])
    probe_out.start()

    def drain(k, carry):
        @pl.when(has_up)
        def _():
            up_copy(k).wait_send()

        @pl.when(has_left & jnp.logical_not(after_seam & on_detour(k)))
        def _():
            side_copy(k).wait_send()

        @pl.when(after_seam & on_detour(k))
        def _():
            detour(k).wait_send()

        @pl.when(before_seam & on_detour(k))
        def _():
            detour_on(k).wait_send()

        @pl.when(passes_on | (has_up & after_seam & jnp.logical_not(even)))
        def _():
            corner_copy(k).wait_send()

        @pl.when(turns_corner)
        def _():
            corner_detour(k).wait_send()

        @pl.when(relays_corner)
        def _():
            corner_detour_on(k).wait_send()

        @pl.when(has_right & jnp.logical_not(before_seam & on_detour(k)))
        def _():
            grad_side(k).wait_send()

        @pl.when(before_seam & on_detour(k))
        def _():
            grad_detour(k).wait_send()
            grad_detour_on(k).wait_send()

        @pl.when(turns_grad_corner)
        def _():
            grad_corner_detour(k).wait_send()

        @pl.when(relays_grad_corner)
        def _():
            grad_corner_detour_on(k).wait_send()

        @pl.when(has_down)
        def _():
            grad_down(k).wait_send()

        @pl.when(has_right & has_down & jnp.logical_not(turns_grad_corner))
        def _():
            grad_corner(k).wait_send()

        out_copy(k).wait()
        return carry

    lax.fori_loop(0, CHUNKS, drain, 0)

    def drain_plane(step, carry):
        plane_copy(step).wait_send()
        gather_copy(step).wait_send()
        return carry

    lax.fori_loop(1, 16, drain_plane, 0)
    for part in range(2):
        z_first(part).wait_send()
        z_second(part).wait_send()
        z_gather_first(part).wait_send()
        z_gather_second(part).wait_send()
        pair_copy(part).wait_send()
        pair_gather(part).wait_send()
    probe_out.wait()


def on_device(object_field, probe_field, offsets, counts, intensity):
    place = offsets.reshape(2 * SLOTS)
    count_row = counts.reshape(COLS)
    measured = intensity.reshape(SLOTS, WIN, WIN)
    row_hi, row_lo = row_tables()
    col_hi, col_lo = column_tables()
    block = (2, WIN, WIN)
    dma = pltpu.SemaphoreType.DMA
    anywhere = pl.BlockSpec(memory_space=pl.ANY)
    scalars = pl.BlockSpec(memory_space=pltpu.SMEM)
    return pl.pallas_call(
        kernel,
        name="ptycho_step",
        out_shape=(
            jax.ShapeDtypeStruct(block, F32), jax.ShapeDtypeStruct(block, F32),
            jax.ShapeDtypeStruct((4,) + block, F32),
        ),
        in_specs=[scalars, scalars] + [anywhere] * 7,
        out_specs=(anywhere, anywhere, anywhere),
        scratch_shapes=[
            pltpu.VMEM(block, F32),
            pltpu.VMEM((3,) + block, F32),
            pltpu.VMEM((4,) + block, F32),
            pltpu.VMEM((3,) + block, F32),
            pltpu.VMEM((SLOTS,) + block, F32),
            pltpu.VMEM((SLOTS,) + block, F32),
            pltpu.VMEM((SLOTS * WIN, 2 * WIN), BF16),
            pltpu.VMEM((SLOTS * WIN, 2 * WIN), BF16),
            pltpu.VMEM((SLOTS, WIN, WIN), BF16),
            pltpu.VMEM((SLOTS, WIN, WIN), BF16),
            pltpu.VMEM((4, SLOTS, WIN, QUARTER), F32),
            pltpu.VMEM((2 * WIN, WIN), BF16),
            pltpu.VMEM((2 * WIN, WIN), BF16),
            pltpu.VMEM((2, 4, 2 * QUARTER, 2 * QUARTER), BF16),
            pltpu.VMEM((2, 4, 2 * QUARTER, 2 * QUARTER), BF16),
            pltpu.VMEM((2 * SLOTS * ROWS, 2 * WIN), BF16),
            pltpu.VMEM((2 * SLOTS * ROWS, 2 * WIN), BF16),
            pltpu.VMEM(block, F32),
            pltpu.VMEM((2, WIN // 2, WIN), F32),
            pltpu.VMEM((2, QUARTER + ROWS, WIN), F32),
            pltpu.VMEM((15, 8, WIN), F32),
            pltpu.VMEM(block, F32),
            dma((10,)), dma((CHUNKS + 1,)),
            dma((CHUNKS,)), dma((CHUNKS,)), dma((CHUNKS,)), dma((CHUNKS,)),
            dma((CHUNKS,)), dma((CHUNKS,)), dma((CHUNKS,)), dma((CHUNKS,)),
            dma((CHUNKS,)), dma((CHUNKS,)), dma((CHUNKS,)), dma((CHUNKS,)),
            dma((CHUNKS,)), dma((CHUNKS,)), dma((CHUNKS,)), dma((CHUNKS,)),
            dma((CHUNKS,)), dma((CHUNKS,)), dma((CHUNKS,)),
            dma((CHUNKS,)), dma((CHUNKS,)), dma((CHUNKS,)),
            dma((2,)), dma((2,)), dma((2, 2)), dma((2, 2)), dma((15,)), dma((15,)),
            dma((15,)), dma((15,)), dma((2, 2)), dma((2, 2)), dma((2,)), dma((2,)),
        ],
        compiler_params=pltpu.CompilerParams(
            collective_id=0, has_side_effects=True, vmem_limit_bytes=62 * 1024 * 1024
        ),
        cost_estimate=pl.CostEstimate(
            flops=20_000_000_000, bytes_accessed=16_000_000, transcendentals=0
        ),
    )(
        place, count_row, object_field, probe_field, measured,
        jnp.asarray(row_hi), jnp.asarray(row_lo), jnp.asarray(col_hi), jnp.asarray(col_lo),
    )[:2]


def solution(mesh):
    placed = (
        P(None, "tile", "pos"),
        P(),
        P("tile", "pos", None, None),
        P("tile", None),
        P("tile", "pos", None, None, None),
    )
    return jax.shard_map(
        on_device,
        mesh=mesh,
        in_specs=placed,
        out_specs=(P(None, "tile", "pos"), P()),
        check_vma=False,
    )
```
